256 devices in a mesh: dp: 8 (over z), seq: 32 (over y, x, core).
Axes of the slice: x: 4, y: 4, z: 8, core: 2. Of those that a mesh axis runs over, the one named last changes fastest.
Arguments:
- gate_input: bfloat16 [8, 4096, 4096], P('dp', 'seq'), may hold values from -6 to 6
- conv_input: bfloat16 [8, 4096, 4096], P('dp', 'seq'), may hold values from -6 to 6
- grad_output: bfloat16 [8, 4096, 4096], P('dp', 'seq'), may hold values from -6 to 6
- filter_taps: bfloat16 [4096, 4096], P('seq'), may hold values from -0.09375 to 0.09375
- block_order: int32 [32], replicated, may hold values from 0 to 31, each once
- owner_rows: int32 [8, 4096], P('dp', 'seq'), may hold values from 0 to 31, as said below
Outputs:
- grad_gate: bfloat16 [8, 4096, 4096], P('dp', 'seq')
- grad_returned: bfloat16 [8, 8192, 4096], P('dp', 'seq')
- grad_filter: float32 [4096, 4096], P('dp', 'seq')
The draws below stay inside these ranges and needn't reach their ends.
Inputs may be any that keep to these rules, and one draw needn't show every extreme that they name: `owner_rows`: in each sequence, no owner is named by more than 8 of the 128 rows of one block, and one owner is named by exactly 8 rows of every block, so that it receives 256 rows. `block_order`: each block number appears once.
All inputs are finite; a program needn't handle non-finite values.
Results may differ from the reference program's by a relative error of at most 0.019.
Values may be sent and summed in bfloat16 or wider, within the bound.
A program may use at most 128 MiB of HBM per device.

```python
import jax
import jax.numpy as jnp
from jax import lax

D = 4096
TOK_DEV = 128
L = 4096
BATCH = 8
SLOT = 8
CAP = 256
N_SEQ = 32


def block_owners(block_key, busiest):
    place_key, owner_key = jax.random.split(block_key)
    positions = jax.random.permutation(place_key, TOK_DEV)
    others = jnp.arange((N_SEQ - 1) * SLOT, dtype=jnp.int32) // SLOT
    others = others + (others >= busiest).astype(jnp.int32)
    others = jax.random.permutation(owner_key, others)[:TOK_DEV - SLOT]
    ordered = jnp.concatenate([jnp.full((SLOT,), busiest, jnp.int32), others])
    return ordered[jnp.argsort(positions)]


def draw_owner_rows(key, part):
    busy_key, remainder = jax.random.split(jax.random.fold_in(key, 7))
    busiest = jax.random.randint(busy_key, (BATCH,), 0, N_SEQ)

    def one_sequence(row_index):
        row_key = jax.random.fold_in(remainder, row_index)

        def one_block(block_index):
            return block_owners(jax.random.fold_in(row_key, block_index), busiest[row_index])
        return jax.vmap(one_block)(jnp.arange(N_SEQ)).reshape(L)
    return jax.vmap(one_sequence)(jnp.arange(BATCH)).astype(jnp.int32)


def steps_of(stream_key, dims, shards, least, largest):
    def one(axis_at, parts):
        draws = jax.random.uniform(jax.random.fold_in(jax.random.fold_in(stream_key, 6), axis_at), (parts,), jnp.float32, least / len(shards), largest / len(shards))
        return jnp.repeat(jnp.exp(draws), dims[axis_at] // parts).reshape((-1,) + (1,) * (len(dims) - axis_at - 1))

    gain = one(*shards[0])
    for cut in shards[1:]:
        gain = gain * one(*cut)
    return gain


def gaussian(stream_key, shape, width, limit, cuts=(), kind=jnp.bfloat16):
    gain = steps_of(stream_key, shape, cuts, -0.22, 0.18) if cuts else 1.0
    result = jax.random.normal(stream_key, shape, jnp.float32) * width * gain
    return jnp.minimum(jnp.maximum(result, -limit), limit).astype(kind)


def setup_inputs(seed: int = 0) -> dict:
    key_list = jax.random.split(jax.random.key(seed), 7)
    gate_input = gaussian(key_list[0], (BATCH, L, D), 1.0, 6.0, ((0, 8), (1, 32)))
    conv_input = gaussian(key_list[1], (BATCH, L, D), 1.0, 6.0, ((0, 8), (1, 32)))
    grad_output = gaussian(key_list[2], (BATCH, L, D), 1.0, 6.0, ((0, 8), (1, 32)))
    filter_taps = gaussian(key_list[3], (L, D), L ** -0.5, 0.09375, ((0, 32),))
    block_order = jax.random.permutation(key_list[4], N_SEQ).astype(jnp.int32)
    owner_rows = draw_owner_rows(jax.random.fold_in(key_list[6], 71), 0)
    return dict(gate_input=gate_input, conv_input=conv_input, grad_output=grad_output, filter_taps=filter_taps, block_order=block_order, owner_rows=owner_rows)


def time_order(rows_cp, inverse):
    blocks = rows_cp.reshape(N_SEQ, TOK_DEV, rows_cp.shape[-1])
    return jnp.take(blocks, inverse, axis=0).reshape(L, rows_cp.shape[-1])


def array_order(rows_time, block_order):
    blocks = rows_time.reshape(N_SEQ, TOK_DEV, rows_time.shape[-1])
    return jnp.take(blocks, block_order, axis=0).reshape(L, rows_time.shape[-1])


def owner_places(owners):
    blocks = owners.reshape(N_SEQ, TOK_DEV)
    owner_ids = jnp.arange(N_SEQ, dtype=jnp.int32)
    owner_hits = (blocks[:, :, None] == owner_ids[None, None, :]).astype(jnp.int32)
    running = jnp.cumsum(owner_hits, axis=1)
    row_rank = jnp.sum(owner_hits * running, axis=2) - 1
    counts = running[:, -1, :]
    starts = jnp.cumsum(counts, axis=0) - counts
    start_of = jnp.sum(owner_hits * starts[:, None, :], axis=2)
    return (blocks * CAP + start_of + row_rank).reshape(L).astype(jnp.int32)


def reference(gate_input, conv_input, grad_output, filter_taps, block_order, owner_rows):
    length = 2 * L
    slot_ids = jnp.arange(N_SEQ, dtype=jnp.int32)
    inverse = jnp.zeros((N_SEQ,), jnp.int32).at[block_order].set(slot_ids)
    taps_spec = jnp.fft.rfft(filter_taps.astype(jnp.float32), n=length, axis=0)

    def one_sequence(carry, inputs):
        gate_rows, conv_rows, upstream, owners = inputs
        mixed_grad = (upstream.astype(jnp.float32) * gate_rows.astype(jnp.float32)).astype(jnp.bfloat16)
        conv_spec = jnp.fft.rfft(time_order(conv_rows, inverse).astype(jnp.float32), n=length, axis=0)
        mixed_spec = jnp.fft.rfft(time_order(mixed_grad, inverse).astype(jnp.float32), n=length, axis=0)
        signal = jnp.fft.irfft(taps_spec * conv_spec, n=length, axis=0)[:L].astype(jnp.bfloat16)
        back_grad = jnp.fft.irfft(jnp.conj(taps_spec) * mixed_spec, n=length, axis=0)[:L].astype(jnp.bfloat16)
        filter_term = jnp.fft.irfft(jnp.conj(conv_spec) * mixed_spec, n=length, axis=0)[:L].astype(jnp.float32)
        signal = array_order(signal, block_order)
        back_grad = array_order(back_grad, block_order)
        grad_gate = (upstream.astype(jnp.float32) * signal.astype(jnp.float32)).astype(jnp.bfloat16)
        places = owner_places(owners)
        returned = jnp.zeros((N_SEQ * CAP, D), jnp.bfloat16).at[places].set(back_grad)
        return carry + filter_term, (grad_gate, returned)

    initial = jnp.zeros((L, D), jnp.float32)
    grad_filter, outputs = lax.scan(one_sequence, initial, (gate_input, conv_input, grad_output, owner_rows))
    return outputs[0], outputs[1], grad_filter
```

```python
import functools
import math

import jax
import jax.numpy as jnp
import numpy as np
from jax import lax
from jax.experimental import pallas as pl
from jax.experimental.pallas import tpu as pltpu
from jax.sharding import PartitionSpec as P

F32, BF16, I32 = jnp.float32, jnp.bfloat16, jnp.int32
MESH = pl.DeviceIdType.MESH
VMEM_BYTES = 60 * 2**20


def spectrum_of(values):
    n = len(values)
    if n == 1:
        return [(values[0], None)]
    even, odd = spectrum_of(values[0::2]), spectrum_of(values[1::2])
    result = [None] * n
    for k in range(n // 2):
        angle = math.pi * (2 * k + 1) / (2 * n)
        c, s = math.cos(angle), -math.sin(angle)
        (er, ei), (hr, hi) = even[k], odd[k]
        if ei is None:
            tr, ti = c * hr, s * hr
            result[k], result[n - 1 - k] = (er + tr, ti), (er - tr, ti)
            continue
        tr, ti = c * hr - s * hi, c * hi + s * hr
        result[k], result[n - 1 - k] = (er + tr, ei + ti), (er - tr, ti - ei)
    return result


def values_of(spectrum):
    n = len(spectrum)
    if n == 1:
        return [spectrum[0][0]]
    even, odd = [], []
    for k in range(n // 2):
        angle = math.pi * (2 * k + 1) / (2 * n)
        c, s = math.cos(angle), math.sin(angle)
        (zr, zi), (pr, pi) = spectrum[k], spectrum[n - 1 - k]
        dr, di = zr - pr, zi + pi
        even.append((zr + pr, zi - pi))
        odd.append((c * dr - s * di, c * di + s * dr))
    result = [None] * n
    result[0::2], result[1::2] = values_of(even), values_of(odd)
    return result


@functools.lru_cache
def tables(blocks, rows):
    k1 = np.arange(blocks)[:, None, None]
    k2 = np.arange(rows)[None, :, None]
    n1 = np.arange(rows)[None, None, :]
    length = 2 * blocks * rows
    phase = (np.pi / length) * ((2 * k1 + 1) * n1 + 2 * blocks * 2 * (k2 * n1 % rows))
    c, s = np.cos(phase), np.sin(phase)
    table = np.concatenate([np.concatenate([c, s], 2), np.concatenate([-s, c], 2)], 1)
    back = np.swapaxes(table, 1, 2) / (blocks * rows)
    return table.astype(jnp.bfloat16), back.astype(jnp.bfloat16)


def kernel(
    n_dp,
    n_seq,
    order,
    place_of,
    owners_in,
    gate,
    conv,
    upstream,
    taps,
    table_in,
    back_in,
    sig_out,
    rows_out,
    parts_out,
    gate_v,
    up_v,
    mixed_v,
    own_got,
    conv_got,
    taps_got,
    mixed_got,
    table,
    back_table,
    pair_a,
    mixed_a,
    specs,
    turned,
    sig_time,
    sig_send,
    back_time,
    starts,
    packed,
    rows_send,
    filt_send,
    send_sem,
    recv_sem,
    local_sem,
):
    dp, seq = lax.axis_index("dp"), lax.axis_index("seq")
    rows = gate_v.shape[0]
    lanes = conv_got.shape[2]
    tile = 16
    slot = rows_send.shape[1] // n_seq

    loads = [
        pltpu.make_async_copy(a, b, local_sem.at[i])
        for i, (a, b) in enumerate(
            ((gate, gate_v), (upstream, up_v), (table_in, table), (back_in, back_table))
        )
    ]
    for load in loads:
        load.start()

    barrier = pltpu.get_barrier_semaphore()

    @pl.loop(1, n_seq)
    def _(hop):
        to = lax.rem(seq + hop, n_seq)
        pl.semaphore_signal(barrier, inc=1, device_id=(dp, to), device_id_type=MESH)

    @pl.loop(1, n_dp)
    def _(hop):
        to = lax.rem(dp + hop, n_dp)
        pl.semaphore_signal(barrier, inc=1, device_id=(to, seq), device_id_type=MESH)

    pl.semaphore_wait(barrier, n_seq - 1 + n_dp - 1)

    def columns(ref, which):
        return ref.at[:, pl.ds(pl.multiple_of(which * lanes, lanes), lanes)]

    def exchange(i, source, target):
        @pl.loop(1, n_seq)
        def _(hop):
            to = lax.rem(seq + hop, n_seq)
            pltpu.make_async_remote_copy(
                src_ref=source(to),
                dst_ref=target,
                send_sem=send_sem.at[i],
                recv_sem=recv_sem.at[i],
                device_id=(dp, to),
                device_id_type=MESH,
            ).start()

        pltpu.make_async_copy(source(seq), target, recv_sem.at[i]).start()

    def arrived(i, ref):
        pltpu.make_async_copy(ref, ref, recv_sem.at[i]).wait()

    def left(i, ref):
        part = ref.at[pl.ds(0, ref.shape[0] - ref.shape[0] // n_seq)]
        pltpu.make_async_copy(part, part, send_sem.at[i]).wait()

    exchange(0, lambda to: owners_in, own_got.at[seq])
    exchange(1, lambda to: columns(conv, to), conv_got.at[seq])
    exchange(2, lambda to: columns(taps, to), taps_got.at[seq])

    loads[0].wait()
    loads[1].wait()

    @pl.loop(0, rows // tile)
    def _(i):
        at = pl.ds(pl.multiple_of(i * tile, tile), tile)
        mixed_v[at, :] = (up_v[at, :].astype(F32) * gate_v[at, :].astype(F32)).astype(BF16)

    exchange(3, lambda to: columns(mixed_v, to), mixed_got.at[seq])

    def transform(got, into, lane, where):
        @pl.loop(0, rows // tile)
        def _(i):
            at = pl.ds(pl.multiple_of(i * tile, tile), tile)
            low = pl.ds(pl.multiple_of(rows + i * tile, tile), tile)
            found = spectrum_of([got[where(q), at, :].astype(F32) for q in range(n_seq)])
            for k in range(n_seq):
                into[k, at, lane : lane + lanes] = found[k][0].astype(BF16)
                into[k, low, lane : lane + lanes] = found[k][1].astype(BF16)

    def invert(lane, put):
        @pl.loop(0, rows // tile)
        def _(i):
            at = pl.ds(pl.multiple_of(i * tile, tile), tile)
            low = pl.ds(pl.multiple_of(rows + i * tile, tile), tile)
            found = values_of(
                [
                    (turned[k, at, lane : lane + lanes], turned[k, low, lane : lane + lanes])
                    for k in range(n_seq)
                ]
            )
            for q in range(n_seq):
                put(q, at, i, found[q].astype(BF16))

    arrived(0, own_got)
    owner_ids = lax.broadcasted_iota(I32, (n_seq, rows), 0)
    wide = lax.broadcasted_iota(I32, (n_seq, n_seq * slot), 1)
    wide_block, wide_slot = wide // slot, wide % slot
    above = lax.broadcasted_iota(I32, (rows, rows), 0)
    beside = lax.broadcasted_iota(I32, (rows, rows), 1)
    earlier = jnp.where(above < beside, 1.0, 0.0).astype(BF16)

    def place(p, carry):
        so_far, first = carry
        hits = jnp.where(own_got[p, 0:1, :] == owner_ids, 1.0, 0.0)
        count = jnp.sum(hits, axis=1, keepdims=True).astype(I32)
        mine = jnp.logical_and(wide_block == p, wide_slot < count)
        return so_far + count, jnp.where(mine, so_far + wide_slot, first)

    _, first = lax.fori_loop(
        0,
        n_seq,
        place,
        (jnp.zeros((n_seq, 1), I32), jnp.full((n_seq, n_seq * slot), -1, I32)),
    )
    starts[...] = first

    arrived(1, conv_got)
    transform(conv_got, pair_a, 0, lambda q: place_of[q])
    arrived(2, taps_got)
    transform(taps_got, pair_a, lanes, lambda q: q)
    loads[2].wait()
    loads[3].wait()

    @pl.loop(0, n_seq)
    def _(k):
        both = jnp.dot(table[k], pair_a[k], preferred_element_type=F32)
        specs[k] = both
        xr, xi = both[:rows, :lanes], both[rows:, :lanes]
        tr, ti = both[:rows, lanes:], both[rows:, lanes:]
        made = jnp.concatenate([xr * tr - xi * ti, xr * ti + xi * tr], axis=0)
        turned[k, :, :lanes] = jnp.dot(
            back_table[k], made.astype(BF16), preferred_element_type=F32
        )

    def put_signal(q, at, i, found):
        sig_time[q, at, :] = found

    invert(0, put_signal)

    @pl.loop(0, n_seq)
    def _(p):
        sig_send[p] = sig_time[order[p]]

    exchange(4, lambda to: sig_send.at[to], columns(sig_out, seq))

    arrived(3, mixed_got)
    transform(mixed_got, mixed_a, 0, lambda q: place_of[q])

    @pl.loop(0, n_seq)
    def _(k):
        mixed = jnp.dot(table[k], mixed_a[k], preferred_element_type=F32)
        mr, mi = mixed[:rows], mixed[rows:]
        xr, xi = specs[k, :rows, :lanes], specs[k, rows:, :lanes]
        tr, ti = specs[k, :rows, lanes:], specs[k, rows:, lanes:]
        made = jnp.concatenate(
            [
                jnp.concatenate([tr * mr + ti * mi, xr * mr + xi * mi], axis=1),
                jnp.concatenate([tr * mi - ti * mr, xr * mi - xi * mr], axis=1),
            ],
            axis=0,
        )
        turned[k] = jnp.dot(back_table[k], made.astype(BF16), preferred_element_type=F32)

    def put_back(q, at, i, found):
        back_time[q, at, :] = found

    invert(0, put_back)

    def pack(p):
        owner = own_got[p, 0:1, :]
        hits = jnp.where(owner == owner_ids, 1.0, 0.0)
        before = jnp.dot(hits.astype(BF16), earlier, preferred_element_type=F32)
        rank = jnp.sum(hits * before, axis=0, keepdims=True).astype(I32)
        place_ids = lax.broadcasted_iota(I32, (n_seq * slot, rows), 0)
        chosen = jnp.where(owner * slot + rank == place_ids, 1.0, 0.0).astype(BF16)
        found = jnp.dot(chosen, back_time[order[p]], preferred_element_type=F32)
        at = pl.ds(pl.multiple_of(p * slot, slot), slot)
        packed[:, at, :] = found.reshape(n_seq, slot, lanes)

    pl.loop(0, n_seq)(pack)

    @pl.loop(0, n_seq)
    def _(o):
        row_ids = lax.broadcasted_iota(I32, (n_seq * slot, n_seq * slot), 0)
        chosen = jnp.where(starts[pl.ds(o, 1), :] == row_ids, 1.0, 0.0).astype(BF16)
        found = jnp.dot(chosen, packed[o].astype(BF16), preferred_element_type=F32)
        rows_send[o] = found.astype(BF16)

    exchange(5, lambda to: rows_send.at[to], columns(rows_out, seq))

    per = n_seq // n_dp

    def put_filter(q, at, i, found):
        down = pl.ds(pl.multiple_of((q % per) * rows + i * tile, tile), tile)
        filt_send[q // per, down, :] = found

    invert(lanes, put_filter)

    @pl.loop(1, n_dp)
    def _(hop):
        to = lax.rem(dp + hop, n_dp)
        pltpu.make_async_remote_copy(
            src_ref=filt_send.at[to],
            dst_ref=parts_out.at[dp],
            send_sem=send_sem.at[6],
            recv_sem=recv_sem.at[6],
            device_id=(to, seq),
            device_id_type=MESH,
        ).start()

    pltpu.make_async_copy(filt_send.at[dp], parts_out.at[dp], recv_sem.at[6]).start()

    left(0, own_got)
    left(1, conv_got)
    left(2, taps_got)
    left(3, mixed_got)
    left(4, sig_send)
    left(5, rows_send)
    others = filt_send.at[pl.ds(0, n_dp - 1)]
    pltpu.make_async_copy(others, others, send_sem.at[6]).wait()
    arrived(4, sig_out)
    arrived(6, parts_out)
    arrived(5, rows_out)


def per_device(gate_input, conv_input, grad_output, filter_taps, block_order, owner_rows):
    gate_rows, conv_rows, upstream = gate_input[0], conv_input[0], grad_output[0]
    rows, channels = gate_rows.shape
    n_dp, n_seq = lax.axis_size("dp"), lax.axis_size("seq")
    lanes = channels // n_seq
    cap = 2 * rows
    slot = cap // n_seq
    ids = jnp.arange(n_seq, dtype=I32)
    place_of = jnp.sum(jnp.where(block_order[None, :] == ids[:, None], ids[None, :], 0), axis=1)
    table, back_table = tables(n_seq, rows)
    anywhere, scalars = pl.BlockSpec(memory_space=pl.ANY), pl.BlockSpec(memory_space=pltpu.SMEM)
    full = (n_seq, rows, lanes)
    scratch = (
        [pltpu.VMEM((rows, channels), BF16)] * 3
        + [pltpu.VMEM((n_seq, 8, rows), I32)]
        + [pltpu.VMEM(full, BF16)] * 3
        + [pltpu.VMEM((n_seq, 2 * rows, 2 * rows), BF16)] * 2
        + [
            pltpu.VMEM((n_seq, 2 * rows, 2 * lanes), BF16),
            pltpu.VMEM((n_seq, 2 * rows, lanes), BF16),
            pltpu.VMEM((n_seq, 2 * rows, 2 * lanes), F32),
            pltpu.VMEM((n_seq, 2 * rows, 2 * lanes), F32),
        ]
        + [pltpu.VMEM(full, BF16)] * 3
        + [
            pltpu.VMEM((n_seq, n_seq * slot), I32),
            pltpu.VMEM((n_seq, n_seq * slot, lanes), F32),
            pltpu.VMEM((n_seq, cap, lanes), BF16),
            pltpu.VMEM((n_dp, n_seq * rows // n_dp, lanes), BF16),
            pltpu.SemaphoreType.DMA((7,)),
            pltpu.SemaphoreType.DMA((7,)),
            pltpu.SemaphoreType.DMA((4,)),
        ]
    )
    signal, returned, parts = pl.pallas_call(
        functools.partial(kernel, n_dp, n_seq),
        out_shape=(
            jax.ShapeDtypeStruct((rows, channels), BF16),
            jax.ShapeDtypeStruct((cap, channels), BF16),
            jax.ShapeDtypeStruct((n_dp, n_seq * rows // n_dp, lanes), BF16),
        ),
        in_specs=[scalars, scalars] + [anywhere] * 7,
        out_specs=(anywhere,) * 3,
        scratch_shapes=scratch,
        compiler_params=pltpu.CompilerParams(
            collective_id=0, has_side_effects=True, vmem_limit_bytes=VMEM_BYTES
        ),
        name="conv_backward",
    )(
        block_order,
        place_of,
        jnp.broadcast_to(owner_rows, (8, rows)),
        gate_rows,
        conv_rows,
        upstream,
        filter_taps,
        jnp.asarray(table),
        jnp.asarray(back_table),
    )
    grad_gate = (upstream.astype(F32) * signal.astype(F32)).astype(BF16)
    grad_filter = jnp.sum(parts.astype(F32), axis=0)
    return grad_gate[None], returned[None], grad_filter


def solution(mesh):
    placed = (
        P("dp", "seq", None),
        P("dp", "seq", None),
        P("dp", "seq", None),
        P("seq", None),
        P(),
        P("dp", "seq"),
    )
    return jax.shard_map(
        per_device,
        mesh=mesh,
        in_specs=placed,
        out_specs=(P("dp", "seq", None), P("dp", "seq", None), P("dp", "seq")),
        check_vma=False,
    )
```

```python
import functools
import math

import jax
import jax.numpy as jnp
import numpy as np
from jax import lax
from jax.experimental import pallas as pl
from jax.experimental.pallas import tpu as pltpu
from jax.sharding import PartitionSpec as P

F32, BF16, I32 = jnp.float32, jnp.bfloat16, jnp.int32
MESH = pl.DeviceIdType.MESH
VMEM_BYTES = 60 * 2**20


def spectrum_of(values):
    n = len(values)
    if n == 1:
        return [(values[0], None)]
    even, odd = spectrum_of(values[0::2]), spectrum_of(values[1::2])
    result = [None] * n
    for k in range(n // 2):
        angle = math.pi * (2 * k + 1) / (2 * n)
        c, s = math.cos(angle), -math.sin(angle)
        (er, ei), (hr, hi) = even[k], odd[k]
        if ei is None:
            tr, ti = c * hr, s * hr
            result[k], result[n - 1 - k] = (er + tr, ti), (er - tr, ti)
            continue
        tr, ti = c * hr - s * hi, c * hi + s * hr
        result[k], result[n - 1 - k] = (er + tr, ei + ti), (er - tr, ti - ei)
    return result


def values_of(spectrum):
    n = len(spectrum)
    if n == 1:
        return [spectrum[0][0]]
    even, odd = [], []
    for k in range(n // 2):
        angle = math.pi * (2 * k + 1) / (2 * n)
        c, s = math.cos(angle), math.sin(angle)
        (zr, zi), (pr, pi) = spectrum[k], spectrum[n - 1 - k]
        dr, di = zr - pr, zi + pi
        even.append((zr + pr, zi - pi))
        odd.append((c * dr - s * di, c * di + s * dr))
    result = [None] * n
    result[0::2], result[1::2] = values_of(even), values_of(odd)
    return result


@functools.lru_cache
def tables(blocks, rows):
    k1 = np.arange(blocks)[:, None, None]
    k2 = np.arange(rows)[None, :, None]
    n1 = np.arange(rows)[None, None, :]
    length = 2 * blocks * rows
    phase = (np.pi / length) * ((2 * k1 + 1) * n1 + 2 * blocks * 2 * (k2 * n1 % rows))
    c, s = np.cos(phase), np.sin(phase)
    table = np.concatenate([np.concatenate([c, s], 2), np.concatenate([-s, c], 2)], 1)
    back = np.swapaxes(table, 1, 2) / (blocks * rows)
    return table.astype(jnp.bfloat16), back.astype(jnp.bfloat16)


def kernel(
    n_dp,
    n_seq,
    order,
    owners_in,
    gate,
    conv,
    upstream,
    taps,
    table_in,
    back_in,
    gate_out,
    rows_out,
    filter_out,
    place_of,
    gate_v,
    up_v,
    mixed_v,
    sig_got,
    own_got,
    conv_got,
    taps_got,
    mixed_got,
    table,
    back_table,
    pair_a,
    specs,
    turned,
    sig_time,
    sig_send,
    back_time,
    starts,
    slot_of,
    row_of,
    packed,
    rows_send,
    filt_send,
    parts_got,
    filt_sum,
    send_sem,
    recv_sem,
    local_sem,
):
    dp, seq = lax.axis_index("dp"), lax.axis_index("seq")
    rows = gate_v.shape[0]
    lanes = conv_got.shape[2]
    tile = 16
    slot = rows_send.shape[1] // n_seq
    side = math.isqrt(n_seq // 2)

    loads = [
        pltpu.make_async_copy(a, b, local_sem.at[i])
        for i, (a, b) in enumerate(
            ((gate, gate_v), (upstream, up_v), (table_in, table), (back_in, back_table))
        )
    ]
    for load in loads:
        load.start()

    barrier = pltpu.get_barrier_semaphore()

    @pl.loop(1, n_seq)
    def _(hop):
        to = lax.rem(seq + hop, n_seq)
        pl.semaphore_signal(barrier, inc=1, device_id=(dp, to), device_id_type=MESH)

    @pl.loop(1, n_dp)
    def _(hop):
        to = lax.rem(dp + hop, n_dp)
        pl.semaphore_signal(barrier, inc=1, device_id=(to, seq), device_id_type=MESH)

    pl.semaphore_wait(barrier, n_seq - 1 + n_dp - 1)

    def columns(ref, which):
        return ref.at[:, pl.ds(pl.multiple_of(which * lanes, lanes), lanes)]

    core, place_x, place_y = seq % 2, seq // 2 % side, seq // (2 * side)
    odd, sign = (place_x + place_y) % 2, 1 - 2 * core

    def partner(hop):
        u, v = hop // 2 % side, hop // (2 * side)
        dx, dy = odd * v + (1 - odd) * u, odd * u + (1 - odd) * v
        y, x = (place_y + side + sign * dy) % side, (place_x + side + sign * dx) % side
        return (y * side + x) * 2 + (core + hop) % 2

    def exchange(i, source, target):
        @pl.loop(1, n_seq)
        def _(hop):
            to = partner(hop)
            pltpu.make_async_remote_copy(
                src_ref=source(to),
                dst_ref=target,
                send_sem=send_sem.at[i],
                recv_sem=recv_sem.at[i],
                device_id=(dp, to),
                device_id_type=MESH,
            ).start()

        pltpu.make_async_copy(source(seq), target, recv_sem.at[i]).start()

    def arrived(i, ref):
        pltpu.make_async_copy(ref, ref, recv_sem.at[i]).wait()

    def left(i, ref):
        part = ref.at[pl.ds(0, ref.shape[0] - ref.shape[0] // n_seq)]
        pltpu.make_async_copy(part, part, send_sem.at[i]).wait()

    exchange(0, lambda to: owners_in, own_got.at[pl.ds(seq, 1)])
    exchange(1, lambda to: columns(conv, to), conv_got.at[seq])
    exchange(2, lambda to: columns(taps, to), taps_got.at[seq])

    loads[0].wait()
    loads[1].wait()

    @pl.loop(0, rows // tile)
    def _(i):
        at = pl.ds(pl.multiple_of(i * tile, tile), tile)
        mixed_v[at, :] = (up_v[at, :].astype(F32) * gate_v[at, :].astype(F32)).astype(BF16)

    exchange(3, lambda to: columns(mixed_v, to), mixed_got.at[seq])

    def transform(got, into, lane, where):
        @pl.loop(0, rows // tile)
        def _(i):
            at = pl.ds(pl.multiple_of(i * tile, tile), tile)
            low = pl.ds(pl.multiple_of(rows + i * tile, tile), tile)
            found = spectrum_of([got[where(q), at, :].astype(F32) for q in range(n_seq)])
            for k in range(n_seq):
                into[k, at, lane : lane + lanes] = found[k][0].astype(BF16)
                into[k, low, lane : lane + lanes] = found[k][1].astype(BF16)

    def invert(lane, put):
        @pl.loop(0, rows // tile)
        def _(i):
            at = pl.ds(pl.multiple_of(i * tile, tile), tile)
            low = pl.ds(pl.multiple_of(rows + i * tile, tile), tile)
            found = values_of(
                [
                    (turned[k, at, lane : lane + lanes], turned[k, low, lane : lane + lanes])
                    for k in range(n_seq)
                ]
            )
            for q in range(n_seq):
                put(q, at, i, found[q].astype(BF16))

    @pl.loop(0, n_seq)
    def _(q):
        found = 0
        for p in range(n_seq):
            found = jnp.where(order[p] == q, p, found)
        place_of[q] = found

    arrived(0, own_got)
    owner_ids = lax.broadcasted_iota(I32, (n_seq, rows), 0)
    wide = lax.broadcasted_iota(I32, (n_seq, n_seq * slot), 1)
    wide_block, wide_slot = wide // slot, wide % slot
    above = lax.broadcasted_iota(I32, (rows, rows), 0)
    beside = lax.broadcasted_iota(I32, (rows, rows), 1)
    earlier = jnp.where(above < beside, 1.0, 0.0).astype(BF16)

    def place(p, carry):
        so_far, first = carry
        owner = own_got[pl.ds(p, 1), :]
        hits = jnp.where(owner == owner_ids, 1.0, 0.0)
        count = jnp.sum(hits, axis=1, keepdims=True).astype(I32)
        mine = jnp.logical_and(wide_block == p, wide_slot < count)
        return so_far + count, jnp.where(mine, so_far + wide_slot, first)

    _, first = lax.fori_loop(
        0,
        n_seq,
        place,
        (jnp.zeros((n_seq, 1), I32), jnp.full((n_seq, n_seq * slot), -1, I32)),
    )
    starts[...] = first

    @pl.loop(0, n_seq, unroll=4)
    def _(p):
        owner = own_got[pl.ds(p, 1), :]
        hits = jnp.where(owner == owner_ids, 1.0, 0.0)
        before = jnp.dot(hits.astype(BF16), earlier, preferred_element_type=F32)
        rank = jnp.sum(hits * before, axis=0, keepdims=True).astype(I32)
        place_ids = lax.broadcasted_iota(I32, (n_seq * slot, rows), 0)
        slot_of[p] = jnp.where(owner * slot + rank == place_ids, 1.0, 0.0).astype(BF16)

    @pl.loop(0, n_seq, unroll=4)
    def _(o):
        row_ids = lax.broadcasted_iota(I32, (n_seq * slot, n_seq * slot), 0)
        row_of[o] = jnp.where(starts[pl.ds(o, 1), :] == row_ids, 1.0, 0.0).astype(BF16)

    arrived(1, conv_got)
    transform(conv_got, pair_a, 0, lambda q: place_of[q])
    arrived(2, taps_got)
    transform(taps_got, pair_a, lanes, lambda q: q)
    loads[2].wait()
    loads[3].wait()

    @pl.loop(0, n_seq, unroll=4)
    def _(k):
        both = jnp.dot(table[k], pair_a[k], preferred_element_type=F32)
        specs[k] = both
        xr, xi = both[:rows, :lanes], both[rows:, :lanes]
        tr, ti = both[:rows, lanes:], both[rows:, lanes:]
        made = jnp.concatenate([xr * tr - xi * ti, xr * ti + xi * tr], axis=0)
        turned[k, :, :lanes] = jnp.dot(
            back_table[k], made.astype(BF16), preferred_element_type=F32
        )

    def put_signal(q, at, i, found):
        sig_time[q, at, :] = found

    invert(0, put_signal)

    @pl.loop(0, n_seq)
    def _(p):
        sig_send[p] = sig_time[order[p]]

    exchange(4, lambda to: sig_send.at[to], columns(sig_got, seq))

    arrived(3, mixed_got)
    transform(mixed_got, pair_a, 0, lambda q: place_of[q])

    @pl.loop(0, n_seq, unroll=4)
    def _(k):
        mixed = jnp.dot(table[k], pair_a[k, :, :lanes], preferred_element_type=F32)
        mr, mi = mixed[:rows], mixed[rows:]
        xr, xi = specs[k, :rows, :lanes], specs[k, rows:, :lanes]
        tr, ti = specs[k, :rows, lanes:], specs[k, rows:, lanes:]
        made = jnp.concatenate(
            [
                jnp.concatenate([tr * mr + ti * mi, xr * mr + xi * mi], axis=1),
                jnp.concatenate([tr * mi - ti * mr, xr * mi - xi * mr], axis=1),
            ],
            axis=0,
        )
        turned[k] = jnp.dot(back_table[k], made.astype(BF16), preferred_element_type=F32)

    def put_back(q, at, i, found):
        back_time[q, at, :] = found

    invert(0, put_back)

    @pl.loop(0, n_seq, unroll=4)
    def _(p):
        found = jnp.dot(slot_of[p], back_time[order[p]], preferred_element_type=F32)
        at = pl.ds(pl.multiple_of(p * slot, slot), slot)
        packed[:, at, :] = found.reshape(n_seq, slot, lanes)

    @pl.loop(0, n_seq, unroll=4)
    def _(o):
        found = jnp.dot(row_of[o], packed[o].astype(BF16), preferred_element_type=F32)
        rows_send[o] = found.astype(BF16)

    exchange(5, lambda to: rows_send.at[to], columns(rows_out, seq))

    per = n_seq // n_dp

    def put_filter(q, at, i, found):
        down = pl.ds(pl.multiple_of((q % per) * rows + i * tile, tile), tile)
        filt_send[q // per, down, :] = found

    invert(lanes, put_filter)

    @pl.loop(1, n_dp)
    def _(hop):
        to = lax.rem(dp + hop, n_dp)
        pltpu.make_async_remote_copy(
            src_ref=filt_send.at[to],
            dst_ref=parts_got.at[dp],
            send_sem=send_sem.at[6],
            recv_sem=recv_sem.at[6],
            device_id=(to, seq),
            device_id_type=MESH,
        ).start()

    pltpu.make_async_copy(filt_send.at[dp], parts_got.at[dp], recv_sem.at[6]).start()

    arrived(4, sig_got)

    @pl.loop(0, rows // tile)
    def _(i):
        at = pl.ds(pl.multiple_of(i * tile, tile), tile)
        gate_v[at, :] = (up_v[at, :].astype(F32) * sig_got[at, :].astype(F32)).astype(BF16)

    gate_copy = pltpu.make_async_copy(gate_v, gate_out, local_sem.at[0])
    gate_copy.start()
    arrived(6, parts_got)

    @pl.loop(0, per * rows // tile)
    def _(i):
        at = pl.ds(pl.multiple_of(i * tile, tile), tile)
        total = parts_got[0, at, :].astype(F32)
        for z in range(1, n_dp):
            total = total + parts_got[z, at, :].astype(F32)
        filt_sum[at, :] = total

    filter_copy = pltpu.make_async_copy(filt_sum, filter_out, local_sem.at[1])
    filter_copy.start()
    left(0, own_got)
    left(1, conv_got)
    left(2, taps_got)
    left(3, mixed_got)
    left(4, sig_send)
    left(5, rows_send)
    others = filt_send.at[pl.ds(0, n_dp - 1)]
    pltpu.make_async_copy(others, others, send_sem.at[6]).wait()
    gate_copy.wait()
    filter_copy.wait()
    arrived(5, rows_out)


def per_device(gate_input, conv_input, grad_output, filter_taps, block_order, owner_rows):
    gate_rows, conv_rows, upstream = gate_input[0], conv_input[0], grad_output[0]
    rows, channels = gate_rows.shape
    n_dp, n_seq = lax.axis_size("dp"), lax.axis_size("seq")
    lanes = channels // n_seq
    cap = 2 * rows
    slot = cap // n_seq
    table, back_table = tables(n_seq, rows)
    anywhere, scalars = pl.BlockSpec(memory_space=pl.ANY), pl.BlockSpec(memory_space=pltpu.SMEM)
    full = (n_seq, rows, lanes)
    square = (n_seq, 2 * rows, 2 * lanes)
    parts = (n_dp, n_seq * rows // n_dp, lanes)
    scratch = [
        pltpu.SMEM((n_seq,), I32),
        *[pltpu.VMEM((rows, channels), BF16)] * 4,
        pltpu.VMEM((n_seq, rows), I32),
        *[pltpu.VMEM(full, BF16)] * 3,
        *[pltpu.VMEM((n_seq, 2 * rows, 2 * rows), BF16)] * 2,
        pltpu.VMEM(square, BF16),
        pltpu.VMEM(square, F32),
        pltpu.VMEM(square, F32),
        *[pltpu.VMEM(full, BF16)] * 3,
        pltpu.VMEM((n_seq, cap), I32),
        pltpu.VMEM((n_seq, cap, rows), BF16),
        pltpu.VMEM((n_seq, cap, cap), BF16),
        pltpu.VMEM((n_seq, cap, lanes), F32),
        pltpu.VMEM((n_seq, cap, lanes), BF16),
        pltpu.VMEM(parts, BF16),
        pltpu.VMEM(parts, BF16),
        pltpu.VMEM(parts[1:], F32),
        pltpu.SemaphoreType.DMA((7,)),
        pltpu.SemaphoreType.DMA((7,)),
        pltpu.SemaphoreType.DMA((4,)),
    ]
    grad_gate, returned, grad_filter = pl.pallas_call(
        functools.partial(kernel, n_dp, n_seq),
        out_shape=(
            jax.ShapeDtypeStruct((rows, channels), BF16),
            jax.ShapeDtypeStruct((cap, channels), BF16),
            jax.ShapeDtypeStruct(parts[1:], F32),
        ),
        in_specs=[scalars] + [anywhere] * 7,
        out_specs=(anywhere,) * 3,
        scratch_shapes=scratch,
        compiler_params=pltpu.CompilerParams(
            collective_id=0, has_side_effects=True, vmem_limit_bytes=VMEM_BYTES
        ),
        name="conv_backward",
    )(
        block_order,
        owner_rows,
        gate_rows,
        conv_rows,
        upstream,
        filter_taps,
        jnp.asarray(table),
        jnp.asarray(back_table),
    )
    return grad_gate[None], returned[None], grad_filter


def solution(mesh):
    placed = (
        P("dp", "seq", None),
        P("dp", "seq", None),
        P("dp", "seq", None),
        P("seq", None),
        P(),
        P("dp", "seq"),
    )
    return jax.shard_map(
        per_device,
        mesh=mesh,
        in_specs=placed,
        out_specs=(P("dp", "seq", None), P("dp", "seq", None), P("dp", "seq")),
        check_vma=False,
    )
```

```python
import functools
import math

import jax
import jax.numpy as jnp
import numpy as np
from jax import lax
from jax.experimental import pallas as pl
from jax.experimental.pallas import tpu as pltpu
from jax.sharding import PartitionSpec as P

F32, BF16, I32 = jnp.float32, jnp.bfloat16, jnp.int32
MESH = pl.DeviceIdType.MESH
VMEM_BYTES = 58 * 2**20


def spectrum_of(values):
    n = len(values)
    if n == 1:
        return [(values[0], None)]
    even, odd = spectrum_of(values[0::2]), spectrum_of(values[1::2])
    result = [None] * n
    for k in range(n // 2):
        angle = math.pi * (2 * k + 1) / (2 * n)
        c, s = math.cos(angle), -math.sin(angle)
        (er, ei), (hr, hi) = even[k], odd[k]
        if ei is None:
            tr, ti = c * hr, s * hr
            result[k], result[n - 1 - k] = (er + tr, ti), (er - tr, ti)
            continue
        tr, ti = c * hr - s * hi, c * hi + s * hr
        result[k], result[n - 1 - k] = (er + tr, ei + ti), (er - tr, ti - ei)
    return result


def values_of(spectrum):
    n = len(spectrum)
    if n == 1:
        return [spectrum[0][0]]
    even, odd = [], []
    for k in range(n // 2):
        angle = math.pi * (2 * k + 1) / (2 * n)
        c, s = math.cos(angle), math.sin(angle)
        (zr, zi), (pr, pi) = spectrum[k], spectrum[n - 1 - k]
        dr, di = zr - pr, zi + pi
        even.append((zr + pr, zi - pi))
        odd.append((c * dr - s * di, c * di + s * dr))
    result = [None] * n
    result[0::2], result[1::2] = values_of(even), values_of(odd)
    return result


@functools.lru_cache
def tables(blocks, rows):
    k1 = np.arange(blocks)[:, None, None]
    k2 = np.arange(rows)[None, :, None]
    n1 = np.arange(rows)[None, None, :]
    length = 2 * blocks * rows
    phase = (np.pi / length) * ((2 * k1 + 1) * n1 + 2 * blocks * 2 * (k2 * n1 % rows))
    c, s = np.cos(phase), np.sin(phase)
    table = np.concatenate([np.concatenate([c, s], 2), np.concatenate([-s, c], 2)], 1)
    back = np.swapaxes(table, 1, 2) / (blocks * rows)
    return table.astype(jnp.bfloat16), back.astype(jnp.bfloat16)


def kernel(
    n_dp,
    n_seq,
    order,
    owners_in,
    gate,
    conv,
    upstream,
    taps,
    table_in,
    back_in,
    gate_out,
    rows_out,
    filter_out,
    place_of,
    gate_v,
    up_v,
    mixed_v,
    sig_got,
    own_got,
    conv_got,
    taps_got,
    mixed_got,
    table,
    back_table,
    pair_a,
    specs,
    turned,
    sig_time,
    sig_send,
    back_time,
    starts,
    slot_of,
    row_of,
    packed,
    rows_send,
    filt_send,
    parts_got,
    send_sem,
    recv_sem,
    local_sem,
    ring_send,
    ring_recv,
):
    dp, seq = lax.axis_index("dp"), lax.axis_index("seq")
    rows = gate_v.shape[0]
    lanes = conv_got.shape[2]
    tile = 16
    slot = rows_send.shape[1] // n_seq
    side = math.isqrt(n_seq // 2)

    loads = [
        pltpu.make_async_copy(a, b, local_sem.at[i])
        for i, (a, b) in enumerate(
            (
                (gate, gate_v),
                (upstream, up_v),
                (table_in, table),
                (back_in, back_table),
            )
        )
    ]
    for load in loads:
        load.start()

    barrier = pltpu.get_barrier_semaphore()

    @pl.loop(1, n_seq)
    def _(hop):
        to = lax.rem(seq + hop, n_seq)
        pl.semaphore_signal(barrier, inc=1, device_id=(dp, to), device_id_type=MESH)

    @pl.loop(1, n_dp)
    def _(hop):
        to = lax.rem(dp + hop, n_dp)
        pl.semaphore_signal(barrier, inc=1, device_id=(to, seq), device_id_type=MESH)

    pl.semaphore_wait(barrier, n_seq - 1 + n_dp - 1)

    def columns(ref, which):
        return ref.at[:, pl.ds(pl.multiple_of(which * lanes, lanes), lanes)]

    core, place_x, place_y = seq % 2, seq // 2 % side, seq // (2 * side)
    odd, sign = (place_x + place_y) % 2, 1 - 2 * core

    def partner(hop):
        u, v = hop // 2 % side, hop // (2 * side)
        dx, dy = odd * v + (1 - odd) * u, odd * u + (1 - odd) * v
        y, x = (place_y + side + sign * dy) % side, (place_x + side + sign * dx) % side
        return (y * side + x) * 2 + (core + hop) % 2

    def exchange(i, source, target):
        @pl.loop(1, n_seq)
        def _(hop):
            to = partner(hop)
            pltpu.make_async_remote_copy(
                src_ref=source(to),
                dst_ref=target,
                send_sem=send_sem.at[i],
                recv_sem=recv_sem.at[i],
                device_id=(dp, to),
                device_id_type=MESH,
            ).start()

        pltpu.make_async_copy(source(seq), target, recv_sem.at[i]).start()

    def arrived(i, ref):
        pltpu.make_async_copy(ref, ref, recv_sem.at[i]).wait()

    def left(i, ref):
        part = ref.at[pl.ds(0, ref.shape[0] - ref.shape[0] // n_seq)]
        pltpu.make_async_copy(part, part, send_sem.at[i]).wait()

    exchange(0, lambda to: owners_in, own_got.at[pl.ds(seq, 1)])
    share = taps.at[pl.ds(pl.multiple_of(dp * tile, tile), tile)]
    exchange(2, lambda to: columns(share, to), taps_got.at[dp, seq])
    exchange(1, lambda to: columns(conv, to), conv_got.at[seq])
    loads[0].wait()
    loads[1].wait()

    @pl.loop(0, rows // tile)
    def _(i):
        at = pl.ds(pl.multiple_of(i * tile, tile), tile)
        mixed_v[at, :] = (up_v[at, :].astype(F32) * gate_v[at, :].astype(F32)).astype(BF16)

    exchange(3, lambda to: columns(mixed_v, to), mixed_got.at[seq])

    def ring(step):
        halves = step == n_dp // 2 - 1
        parts = (pl.ds(0, n_seq // 2), pl.ds(n_seq // 2, n_seq // 2)) if halves else (pl.ds(0, n_seq),) * 2
        copies = []
        for way, turn in enumerate((1, -1)):
            held = taps_got.at[lax.rem(dp - turn * step + n_dp, n_dp), parts[way]]
            copies.append(
                pltpu.make_async_remote_copy(
                    src_ref=held,
                    dst_ref=held,
                    send_sem=ring_send.at[2 * step + way],
                    recv_sem=ring_recv.at[2 * step + way],
                    device_id=(lax.rem(dp + turn + n_dp, n_dp), seq),
                    device_id_type=MESH,
                )
            )
        return copies

    rings = [ring(step) for step in range(n_dp // 2)]

    def send_on(step):
        for copy in rings[step]:
            copy.start()

    def met(step):
        for copy in rings[step]:
            copy.wait_recv()

    arrived(2, taps_got.at[dp])
    send_on(0)

    def transform(load, into, lane):
        @pl.loop(0, rows // tile)
        def _(i):
            at = pl.ds(pl.multiple_of(i * tile, tile), tile)
            low = pl.ds(pl.multiple_of(rows + i * tile, tile), tile)
            found = spectrum_of([load(q, at, i).astype(F32) for q in range(n_seq)])
            for k in range(n_seq):
                into[k, at, lane : lane + lanes] = found[k][0].astype(BF16)
                into[k, low, lane : lane + lanes] = found[k][1].astype(BF16)

    def invert(lane, put):
        @pl.loop(0, rows // tile)
        def _(i):
            at = pl.ds(pl.multiple_of(i * tile, tile), tile)
            low = pl.ds(pl.multiple_of(rows + i * tile, tile), tile)
            found = values_of(
                [
                    (turned[k, at, lane : lane + lanes], turned[k, low, lane : lane + lanes])
                    for k in range(n_seq)
                ]
            )
            for q in range(n_seq):
                put(q, at, i, found[q].astype(BF16))

    @pl.loop(0, n_seq)
    def _(q):
        found = 0
        for p in range(n_seq):
            found = jnp.where(order[p] == q, p, found)
        place_of[q] = found

    arrived(0, own_got)
    owner_ids = lax.broadcasted_iota(I32, (n_seq, rows), 0)
    wide = lax.broadcasted_iota(I32, (n_seq, n_seq * slot), 1)
    wide_block, wide_slot = wide // slot, wide % slot
    above = lax.broadcasted_iota(I32, (rows, rows), 0)
    beside = lax.broadcasted_iota(I32, (rows, rows), 1)
    earlier = jnp.where(above < beside, 1.0, 0.0).astype(BF16)

    def place(p, carry):
        so_far, first = carry
        owner = own_got[pl.ds(p, 1), :]
        hits = jnp.where(owner == owner_ids, 1.0, 0.0)
        count = jnp.sum(hits, axis=1, keepdims=True).astype(I32)
        mine = jnp.logical_and(wide_block == p, wide_slot < count)
        return so_far + count, jnp.where(mine, so_far + wide_slot, first)

    _, first = lax.fori_loop(
        0,
        n_seq,
        place,
        (jnp.zeros((n_seq, 1), I32), jnp.full((n_seq, n_seq * slot), -1, I32)),
    )
    starts[...] = first
    met(0)
    send_on(1)

    @pl.loop(0, n_seq, unroll=4)
    def _(p):
        owner = own_got[pl.ds(p, 1), :]
        hits = jnp.where(owner == owner_ids, 1.0, 0.0)
        before = jnp.dot(hits.astype(BF16), earlier, preferred_element_type=F32)
        rank = jnp.sum(hits * before, axis=0, keepdims=True).astype(I32)
        place_ids = lax.broadcasted_iota(I32, (n_seq * slot, rows), 0)
        slot_of[p] = jnp.where(owner * slot + rank == place_ids, 1.0, 0.0).astype(BF16)

    met(1)
    send_on(2)

    @pl.loop(0, n_seq, unroll=4)
    def _(o):
        row_ids = lax.broadcasted_iota(I32, (n_seq * slot, n_seq * slot), 0)
        row_of[o] = jnp.where(starts[pl.ds(o, 1), :] == row_ids, 1.0, 0.0).astype(BF16)

    met(2)
    send_on(3)
    arrived(1, conv_got)
    transform(lambda q, at, i: conv_got[place_of[q], at, :], pair_a, 0)
    met(3)
    transform(lambda q, at, i: taps_got[i, q], pair_a, lanes)
    loads[2].wait()
    loads[3].wait()

    @pl.loop(0, n_seq, unroll=4)
    def _(k):
        both = jnp.dot(table[k], pair_a[k], preferred_element_type=F32)
        specs[k] = both
        xr, xi = both[:rows, :lanes], both[rows:, :lanes]
        tr, ti = both[:rows, lanes:], both[rows:, lanes:]
        made = jnp.concatenate([xr * tr - xi * ti, xr * ti + xi * tr], axis=0)
        turned[k, :, :lanes] = jnp.dot(
            back_table[k], made.astype(BF16), preferred_element_type=F32
        )

    def put_signal(q, at, i, found):
        sig_time[q, at, :] = found

    invert(0, put_signal)

    @pl.loop(0, n_seq)
    def _(p):
        sig_send[p] = sig_time[order[p]]

    exchange(4, lambda to: sig_send.at[to], columns(sig_got, seq))

    arrived(3, mixed_got)
    transform(lambda q, at, i: mixed_got[place_of[q], at, :], pair_a, 0)

    @pl.loop(0, n_seq, unroll=4)
    def _(k):
        mixed = jnp.dot(table[k], pair_a[k, :, :lanes], preferred_element_type=F32)
        mr, mi = mixed[:rows], mixed[rows:]
        xr, xi = specs[k, :rows, :lanes], specs[k, rows:, :lanes]
        tr, ti = specs[k, :rows, lanes:], specs[k, rows:, lanes:]
        made = jnp.concatenate(
            [
                jnp.concatenate([tr * mr + ti * mi, xr * mr + xi * mi], axis=1),
                jnp.concatenate([tr * mi - ti * mr, xr * mi - xi * mr], axis=1),
            ],
            axis=0,
        )
        turned[k] = jnp.dot(back_table[k], made.astype(BF16), preferred_element_type=F32)

    def put_back(q, at, i, found):
        back_time[q, at, :] = found

    invert(0, put_back)

    @pl.loop(0, n_seq, unroll=4)
    def _(p):
        found = jnp.dot(slot_of[p], back_time[order[p]], preferred_element_type=F32)
        at = pl.ds(pl.multiple_of(p * slot, slot), slot)
        packed[:, at, :] = found.reshape(n_seq, slot, lanes)

    @pl.loop(0, n_seq, unroll=4)
    def _(o):
        found = jnp.dot(row_of[o], packed[o].astype(BF16), preferred_element_type=F32)
        rows_send[o] = found.astype(BF16)

    exchange(5, lambda to: rows_send.at[to], columns(rows_out, seq))

    per = n_seq // n_dp

    def put_filter(q, at, i, found):
        down = pl.ds(pl.multiple_of((q % per) * rows + i * tile, tile), tile)
        filt_send[q // per, down, :] = found

    invert(lanes, put_filter)

    @pl.loop(1, n_dp)
    def _(hop):
        to = lax.rem(dp + hop, n_dp)
        pltpu.make_async_remote_copy(
            src_ref=filt_send.at[to],
            dst_ref=parts_got.at[dp],
            send_sem=send_sem.at[6],
            recv_sem=recv_sem.at[6],
            device_id=(to, seq),
            device_id_type=MESH,
        ).start()

    pltpu.make_async_copy(filt_send.at[dp], parts_got.at[dp], recv_sem.at[6]).start()

    arrived(4, sig_got)

    @pl.loop(0, rows // tile)
    def _(i):
        at = pl.ds(pl.multiple_of(i * tile, tile), tile)
        gate_out[at, :] = (up_v[at, :].astype(F32) * sig_got[at, :].astype(F32)).astype(BF16)

    arrived(6, parts_got)

    @pl.loop(0, per * rows // tile)
    def _(i):
        at = pl.ds(pl.multiple_of(i * tile, tile), tile)
        total = parts_got[0, at, :].astype(F32)
        for z in range(1, n_dp):
            total = total + parts_got[z, at, :].astype(F32)
        filter_out[at, :] = total

    left(0, own_got)
    left(1, conv_got)
    left(2, taps_got.at[dp])
    for copies in rings:
        for copy in copies:
            copy.wait_send()
    left(3, mixed_got)
    left(4, sig_send)
    left(5, rows_send)
    others = filt_send.at[pl.ds(0, n_dp - 1)]
    pltpu.make_async_copy(others, others, send_sem.at[6]).wait()
    arrived(5, rows_out)


def per_device(gate_input, conv_input, grad_output, filter_taps, block_order, owner_rows):
    gate_rows, conv_rows, upstream = gate_input[0], conv_input[0], grad_output[0]
    rows, channels = gate_rows.shape
    n_dp, n_seq = lax.axis_size("dp"), lax.axis_size("seq")
    lanes = channels // n_seq
    cap = 2 * rows
    slot = cap // n_seq
    table, back_table = tables(n_seq, rows)
    anywhere, scalars = pl.BlockSpec(memory_space=pl.ANY), pl.BlockSpec(memory_space=pltpu.SMEM)
    full = (n_seq, rows, lanes)
    square = (n_seq, 2 * rows, 2 * lanes)
    parts = (n_dp, n_seq * rows // n_dp, lanes)
    scratch = [
        pltpu.SMEM((n_seq,), I32),
        *[pltpu.VMEM((rows, channels), BF16)] * 4,
        pltpu.VMEM((n_seq, rows), I32),
        pltpu.VMEM(full, BF16),
        pltpu.VMEM((n_dp, n_seq, rows // n_dp, lanes), BF16),
        pltpu.VMEM(full, BF16),
        *[pltpu.VMEM((n_seq, 2 * rows, 2 * rows), BF16)] * 2,
        pltpu.VMEM(square, BF16),
        pltpu.VMEM(square, F32),
        pltpu.VMEM(square, F32),
        *[pltpu.VMEM(full, BF16)] * 3,
        pltpu.VMEM((n_seq, cap), I32),
        pltpu.VMEM((n_seq, cap, rows), BF16),
        pltpu.VMEM((n_seq, cap, cap), BF16),
        pltpu.VMEM((n_seq, cap, lanes), F32),
        pltpu.VMEM((n_seq, cap, lanes), BF16),
        pltpu.VMEM(parts, BF16),
        pltpu.VMEM(parts, BF16),
        pltpu.SemaphoreType.DMA((7,)),
        pltpu.SemaphoreType.DMA((7,)),
        pltpu.SemaphoreType.DMA((4,)),
        pltpu.SemaphoreType.DMA((n_dp,)),
        pltpu.SemaphoreType.DMA((n_dp,)),
    ]
    grad_gate, returned, grad_filter = pl.pallas_call(
        functools.partial(kernel, n_dp, n_seq),
        out_shape=(
            pltpu.VMEM((rows, channels), BF16),
            pltpu.VMEM((cap, channels), BF16),
            pltpu.VMEM(parts[1:], F32),
        ),
        in_specs=[scalars] + [anywhere] * 7,
        out_specs=(pl.BlockSpec(memory_space=pltpu.VMEM),) * 3,
        scratch_shapes=scratch,
        compiler_params=pltpu.CompilerParams(
            collective_id=0, has_side_effects=True, vmem_limit_bytes=VMEM_BYTES
        ),
        name="conv_backward",
    )(
        block_order,
        owner_rows,
        gate_rows,
        conv_rows,
        upstream,
        filter_taps,
        jnp.asarray(table),
        jnp.asarray(back_table),
    )
    return grad_gate[None], returned[None], grad_filter


def solution(mesh):
    placed = (
        P("dp", "seq", None),
        P("dp", "seq", None),
        P("dp", "seq", None),
        P("seq", None),
        P(),
        P("dp", "seq"),
    )
    return jax.shard_map(
        per_device,
        mesh=mesh,
        in_specs=placed,
        out_specs=(P("dp", "seq", None), P("dp", "seq", None), P("dp", "seq")),
        check_vma=False,
    )
```

```python
import functools
import math

import jax
import jax.numpy as jnp
import numpy as np
from jax import lax
from jax.experimental import pallas as pl
from jax.experimental.pallas import tpu as pltpu
from jax.sharding import PartitionSpec as P

F32, BF16, I32 = jnp.float32, jnp.bfloat16, jnp.int32
MESH = pl.DeviceIdType.MESH
VMEM_BYTES = 58 * 2**20


def spectrum_of(values):
    n = len(values)
    if n == 1:
        return [(values[0], None)]
    even, odd = spectrum_of(values[0::2]), spectrum_of(values[1::2])
    result = [None] * n
    for k in range(n // 2):
        angle = math.pi * (2 * k + 1) / (2 * n)
        c, s = math.cos(angle), -math.sin(angle)
        (er, ei), (hr, hi) = even[k], odd[k]
        if ei is None:
            tr, ti = c * hr, s * hr
            result[k], result[n - 1 - k] = (er + tr, ti), (er - tr, ti)
            continue
        tr, ti = c * hr - s * hi, c * hi + s * hr
        result[k], result[n - 1 - k] = (er + tr, ei + ti), (er - tr, ti - ei)
    return result


def values_of(spectrum):
    n = len(spectrum)
    if n == 1:
        return [spectrum[0][0]]
    even, odd = [], []
    for k in range(n // 2):
        angle = math.pi * (2 * k + 1) / (2 * n)
        c, s = math.cos(angle), math.sin(angle)
        (zr, zi), (pr, pi) = spectrum[k], spectrum[n - 1 - k]
        dr, di = zr - pr, zi + pi
        even.append((zr + pr, zi - pi))
        odd.append((c * dr - s * di, c * di + s * dr))
    result = [None] * n
    result[0::2], result[1::2] = values_of(even), values_of(odd)
    return result


@functools.lru_cache
def tables(blocks, rows):
    k1 = np.arange(blocks)[:, None, None]
    k2 = np.arange(rows)[None, :, None]
    n1 = np.arange(rows)[None, None, :]
    length = 2 * blocks * rows
    phase = (np.pi / length) * ((2 * k1 + 1) * n1 + 2 * blocks * 2 * (k2 * n1 % rows))
    c, s = np.cos(phase), np.sin(phase)
    table = np.concatenate([np.concatenate([c, s], 2), np.concatenate([-s, c], 2)], 1)
    back = np.swapaxes(table, 1, 2) / (blocks * rows)
    return table.astype(jnp.bfloat16), back.astype(jnp.bfloat16)


def kernel(
    n_dp,
    n_seq,
    order,
    owners_in,
    gate,
    conv,
    upstream,
    taps,
    table_in,
    back_in,
    gate_out,
    rows_out,
    filter_out,
    place_of,
    gate_v,
    up_v,
    mixed_v,
    sig_got,
    own_got,
    conv_got,
    taps_got,
    mixed_got,
    table,
    back_table,
    pair_a,
    specs,
    turned,
    sig_time,
    sig_send,
    back_time,
    starts,
    slot_of,
    row_of,
    packed,
    rows_send,
    filt_send,
    parts_got,
    send_sem,
    recv_sem,
    local_sem,
    ring_send,
    ring_recv,
):
    dp, seq = lax.axis_index("dp"), lax.axis_index("seq")
    rows = gate_v.shape[0]
    lanes = conv_got.shape[2]
    tile = 16
    slot = rows_send.shape[1] // n_seq
    side = math.isqrt(n_seq // 2)

    loads = [
        pltpu.make_async_copy(a, b, local_sem.at[i])
        for i, (a, b) in enumerate(
            (
                (gate, gate_v),
                (upstream, up_v),
                (table_in, table),
                (back_in, back_table),
            )
        )
    ]
    for load in loads:
        load.start()

    barrier = pltpu.get_barrier_semaphore()

    @pl.loop(1, n_seq)
    def _(hop):
        to = lax.rem(seq + hop, n_seq)
        pl.semaphore_signal(barrier, inc=1, device_id=(dp, to), device_id_type=MESH)

    @pl.loop(1, n_dp)
    def _(hop):
        to = lax.rem(dp + hop, n_dp)
        pl.semaphore_signal(barrier, inc=1, device_id=(to, seq), device_id_type=MESH)

    pl.semaphore_wait(barrier, n_seq - 1 + n_dp - 1)

    def columns(ref, which):
        return ref.at[:, pl.ds(pl.multiple_of(which * lanes, lanes), lanes)]

    core, place_x, place_y = seq % 2, seq // 2 % side, seq // (2 * side)
    odd, sign = (place_x + place_y) % 2, 1 - 2 * core

    def partner(hop):
        u, v = hop // 2 % side, hop // (2 * side)
        dx, dy = odd * v + (1 - odd) * u, odd * u + (1 - odd) * v
        y, x = (place_y + side + sign * dy) % side, (place_x + side + sign * dx) % side
        return (y * side + x) * 2 + (core + hop) % 2

    def remote(i, source, target, to):
        return pltpu.make_async_remote_copy(
            src_ref=source,
            dst_ref=target,
            send_sem=send_sem.at[i],
            recv_sem=recv_sem.at[i],
            device_id=(dp, to),
            device_id_type=MESH,
        )

    def exchange(i, source, target):
        @pl.loop(1, n_seq)
        def _(hop):
            to = partner(hop)
            remote(i, source(to), target, to).start()

        pltpu.make_async_copy(source(seq), target, recv_sem.at[i]).start()

    def arrived(i, ref):
        pltpu.make_async_copy(ref, ref, recv_sem.at[i]).wait()

    def left(i, ref):
        part = ref.at[pl.ds(0, ref.shape[0] - ref.shape[0] // n_seq)]
        pltpu.make_async_copy(part, part, send_sem.at[i]).wait()

    exchange(0, lambda to: owners_in, own_got.at[pl.ds(seq, 1)])
    share = taps.at[pl.ds(pl.multiple_of(dp * tile, tile), tile)]
    exchange(2, lambda to: columns(share, to), taps_got.at[dp, seq])
    exchange(1, lambda to: columns(conv, to), conv_got.at[seq])
    loads[0].wait()
    loads[1].wait()

    @pl.loop(0, rows // tile)
    def _(i):
        at = pl.ds(pl.multiple_of(i * tile, tile), tile)
        mixed_v[at, :] = (up_v[at, :].astype(F32) * gate_v[at, :].astype(F32)).astype(BF16)

    exchange(3, lambda to: columns(mixed_v, to), mixed_got.at[seq])

    def ring(step):
        halves = step == n_dp // 2 - 1
        parts = (pl.ds(0, n_seq // 2), pl.ds(n_seq // 2, n_seq // 2)) if halves else (pl.ds(0, n_seq),) * 2
        copies = []
        for way, turn in enumerate((1, -1)):
            held = taps_got.at[lax.rem(dp - turn * step + n_dp, n_dp), parts[way]]
            copies.append(
                pltpu.make_async_remote_copy(
                    src_ref=held,
                    dst_ref=held,
                    send_sem=ring_send.at[2 * step + way],
                    recv_sem=ring_recv.at[2 * step + way],
                    device_id=(lax.rem(dp + turn + n_dp, n_dp), seq),
                    device_id_type=MESH,
                )
            )
        return copies

    rings = [ring(step) for step in range(n_dp // 2)]

    def send_on(step):
        for copy in rings[step]:
            copy.start()

    def met(step):
        for copy in rings[step]:
            copy.wait_recv()

    arrived(2, taps_got.at[dp])
    send_on(0)

    def transform(load, into, lane):
        @pl.loop(0, rows // tile)
        def _(i):
            at = pl.ds(pl.multiple_of(i * tile, tile), tile)
            low = pl.ds(pl.multiple_of(rows + i * tile, tile), tile)
            found = spectrum_of([load(q, at, i).astype(F32) for q in range(n_seq)])
            for k in range(n_seq):
                into[k, at, lane : lane + lanes] = found[k][0].astype(BF16)
                into[k, low, lane : lane + lanes] = found[k][1].astype(BF16)

    def invert(lane, put):
        @pl.loop(0, rows // tile)
        def _(i):
            at = pl.ds(pl.multiple_of(i * tile, tile), tile)
            low = pl.ds(pl.multiple_of(rows + i * tile, tile), tile)
            found = values_of(
                [
                    (turned[k, at, lane : lane + lanes], turned[k, low, lane : lane + lanes])
                    for k in range(n_seq)
                ]
            )
            for q in range(n_seq):
                put(q, at, i, found[q].astype(BF16))

    @pl.loop(0, n_seq)
    def _(q):
        found = 0
        for p in range(n_seq):
            found = jnp.where(order[p] == q, p, found)
        place_of[q] = found

    arrived(0, own_got)
    owner_ids = lax.broadcasted_iota(I32, (n_seq, rows), 0)
    wide = lax.broadcasted_iota(I32, (n_seq, n_seq * slot), 1)
    wide_block, wide_slot = wide // slot, wide % slot
    above = lax.broadcasted_iota(I32, (rows, rows), 0)
    beside = lax.broadcasted_iota(I32, (rows, rows), 1)
    earlier = jnp.where(above < beside, 1.0, 0.0).astype(BF16)

    def place(p, carry):
        so_far, first = carry
        owner = own_got[pl.ds(p, 1), :]
        hits = jnp.where(owner == owner_ids, 1.0, 0.0)
        count = jnp.sum(hits, axis=1, keepdims=True).astype(I32)
        mine = jnp.logical_and(wide_block == p, wide_slot < count)
        return so_far + count, jnp.where(mine, so_far + wide_slot, first)

    _, first = lax.fori_loop(
        0,
        n_seq,
        place,
        (jnp.zeros((n_seq, 1), I32), jnp.full((n_seq, n_seq * slot), -1, I32)),
    )
    starts[...] = first
    met(0)
    send_on(1)

    @pl.loop(0, n_seq, unroll=4)
    def _(p):
        owner = own_got[pl.ds(p, 1), :]
        hits = jnp.where(owner == owner_ids, 1.0, 0.0)
        before = jnp.dot(hits.astype(BF16), earlier, preferred_element_type=F32)
        rank = jnp.sum(hits * before, axis=0, keepdims=True).astype(I32)
        place_ids = lax.broadcasted_iota(I32, (n_seq * slot, rows), 0)
        slot_of[p] = jnp.where(owner * slot + rank == place_ids, 1.0, 0.0).astype(BF16)

    met(1)
    send_on(2)

    @pl.loop(0, n_seq, unroll=4)
    def _(o):
        row_ids = lax.broadcasted_iota(I32, (n_seq * slot, n_seq * slot), 0)
        row_of[o] = jnp.where(starts[pl.ds(o, 1), :] == row_ids, 1.0, 0.0).astype(BF16)

    met(2)
    send_on(3)
    arrived(1, conv_got)
    transform(lambda q, at, i: conv_got[place_of[q], at, :], pair_a, 0)
    met(3)
    transform(lambda q, at, i: taps_got[i, q], pair_a, lanes)
    loads[2].wait()
    loads[3].wait()

    @pl.loop(0, n_seq, unroll=16)
    def _(k):
        both = jnp.dot(table[k], pair_a[k], preferred_element_type=F32)
        specs[k] = both
        xr, xi = both[:rows, :lanes], both[rows:, :lanes]
        tr, ti = both[:rows, lanes:], both[rows:, lanes:]
        made = jnp.concatenate([xr * tr - xi * ti, xr * ti + xi * tr], axis=0)
        turned[k, :, :lanes] = jnp.dot(
            back_table[k], made.astype(BF16), preferred_element_type=F32
        )

    def put_signal(q, at, i, found):
        sig_time[q, at, :] = found

    invert(0, put_signal)

    @pl.loop(0, n_seq)
    def _(p):
        sig_send[p] = sig_time[order[p]]

    exchange(4, lambda to: sig_send.at[to], columns(sig_got, seq))

    arrived(3, mixed_got)
    transform(lambda q, at, i: mixed_got[place_of[q], at, :], pair_a, 0)

    @pl.loop(0, n_seq, unroll=16)
    def _(k):
        mixed = jnp.dot(table[k], pair_a[k, :, :lanes], preferred_element_type=F32)
        mr, mi = mixed[:rows], mixed[rows:]
        xr, xi = specs[k, :rows, :lanes], specs[k, rows:, :lanes]
        tr, ti = specs[k, :rows, lanes:], specs[k, rows:, lanes:]
        made = jnp.concatenate(
            [
                jnp.concatenate([tr * mr + ti * mi, xr * mr + xi * mi], axis=1),
                jnp.concatenate([tr * mi - ti * mr, xr * mi - xi * mr], axis=1),
            ],
            axis=0,
        )
        turned[k] = jnp.dot(back_table[k], made.astype(BF16), preferred_element_type=F32)

    def put_back(q, at, i, found):
        back_time[q, at, :] = found

    invert(0, put_back)

    @pl.loop(0, n_seq, unroll=8)
    def _(p):
        found = jnp.dot(slot_of[p], back_time[order[p]], preferred_element_type=F32)
        at = pl.ds(pl.multiple_of(p * slot, slot), slot)
        packed[:, at, :] = found.reshape(n_seq, slot, lanes)

    together = 8

    @pl.loop(0, n_seq // together)
    def _(group):
        partners = [partner(group * together + step) for step in range(together)]
        for to in partners:
            found = jnp.dot(row_of[to], packed[to].astype(BF16), preferred_element_type=F32)
            rows_send[to] = found.astype(BF16)
        for step, to in enumerate(partners):
            copy = remote(5, rows_send.at[to], columns(rows_out, seq), to)
            if step:
                copy.start()
                continue
            pl.when(group > 0)(copy.start)

            @pl.when(group == 0)
            def _():
                own = rows_send.at[seq]
                pltpu.make_async_copy(own, columns(rows_out, seq), recv_sem.at[5]).start()

    per = n_seq // n_dp

    def put_filter(q, at, i, found):
        down = pl.ds(pl.multiple_of((q % per) * rows + i * tile, tile), tile)
        filt_send[q // per, down, :] = found

    invert(lanes, put_filter)

    @pl.loop(1, n_dp)
    def _(hop):
        to = lax.rem(dp + hop, n_dp)
        pltpu.make_async_remote_copy(
            src_ref=filt_send.at[to],
            dst_ref=parts_got.at[dp],
            send_sem=send_sem.at[6],
            recv_sem=recv_sem.at[6],
            device_id=(to, seq),
            device_id_type=MESH,
        ).start()

    pltpu.make_async_copy(filt_send.at[dp], parts_got.at[dp], recv_sem.at[6]).start()

    arrived(4, sig_got)

    @pl.loop(0, rows // tile)
    def _(i):
        at = pl.ds(pl.multiple_of(i * tile, tile), tile)
        gate_out[at, :] = (up_v[at, :].astype(F32) * sig_got[at, :].astype(F32)).astype(BF16)

    arrived(6, parts_got)

    @pl.loop(0, per * rows // tile)
    def _(i):
        at = pl.ds(pl.multiple_of(i * tile, tile), tile)
        total = parts_got[0, at, :].astype(F32)
        for z in range(1, n_dp):
            total = total + parts_got[z, at, :].astype(F32)
        filter_out[at, :] = total

    left(0, own_got)
    left(1, conv_got)
    left(2, taps_got.at[dp])
    for copies in rings:
        for copy in copies:
            copy.wait_send()
    left(3, mixed_got)
    left(4, sig_send)
    left(5, rows_send)
    others = filt_send.at[pl.ds(0, n_dp - 1)]
    pltpu.make_async_copy(others, others, send_sem.at[6]).wait()
    arrived(5, rows_out)


def per_device(gate_input, conv_input, grad_output, filter_taps, block_order, owner_rows):
    gate_rows, conv_rows, upstream = gate_input[0], conv_input[0], grad_output[0]
    rows, channels = gate_rows.shape
    n_dp, n_seq = lax.axis_size("dp"), lax.axis_size("seq")
    lanes = channels // n_seq
    cap = 2 * rows
    slot = cap // n_seq
    table, back_table = tables(n_seq, rows)
    anywhere, scalars = pl.BlockSpec(memory_space=pl.ANY), pl.BlockSpec(memory_space=pltpu.SMEM)
    full = (n_seq, rows, lanes)
    square = (n_seq, 2 * rows, 2 * lanes)
    parts = (n_dp, n_seq * rows // n_dp, lanes)
    scratch = [
        pltpu.SMEM((n_seq,), I32),
        *[pltpu.VMEM((rows, channels), BF16)] * 4,
        pltpu.VMEM((n_seq, rows), I32),
        pltpu.VMEM(full, BF16),
        pltpu.VMEM((n_dp, n_seq, rows // n_dp, lanes), BF16),
        pltpu.VMEM(full, BF16),
        *[pltpu.VMEM((n_seq, 2 * rows, 2 * rows), BF16)] * 2,
        pltpu.VMEM(square, BF16),
        pltpu.VMEM(square, F32),
        pltpu.VMEM(square, F32),
        *[pltpu.VMEM(full, BF16)] * 3,
        pltpu.VMEM((n_seq, cap), I32),
        pltpu.VMEM((n_seq, cap, rows), BF16),
        pltpu.VMEM((n_seq, cap, cap), BF16),
        pltpu.VMEM((n_seq, cap, lanes), F32),
        pltpu.VMEM((n_seq, cap, lanes), BF16),
        pltpu.VMEM(parts, BF16),
        pltpu.VMEM(parts, BF16),
        pltpu.SemaphoreType.DMA((7,)),
        pltpu.SemaphoreType.DMA((7,)),
        pltpu.SemaphoreType.DMA((4,)),
        pltpu.SemaphoreType.DMA((n_dp,)),
        pltpu.SemaphoreType.DMA((n_dp,)),
    ]
    grad_gate, returned, grad_filter = pl.pallas_call(
        functools.partial(kernel, n_dp, n_seq),
        out_shape=(
            pltpu.VMEM((rows, channels), BF16),
            pltpu.VMEM((cap, channels), BF16),
            pltpu.VMEM(parts[1:], F32),
        ),
        in_specs=[scalars] + [anywhere] * 7,
        out_specs=(pl.BlockSpec(memory_space=pltpu.VMEM),) * 3,
        scratch_shapes=scratch,
        compiler_params=pltpu.CompilerParams(
            collective_id=0, has_side_effects=True, vmem_limit_bytes=VMEM_BYTES
        ),
        name="conv_backward",
    )(
        block_order,
        owner_rows,
        gate_rows,
        conv_rows,
        upstream,
        filter_taps,
        jnp.asarray(table),
        jnp.asarray(back_table),
    )
    return grad_gate[None], returned[None], grad_filter


def solution(mesh):
    placed = (
        P("dp", "seq", None),
        P("dp", "seq", None),
        P("dp", "seq", None),
        P("seq", None),
        P(),
        P("dp", "seq"),
    )
    return jax.shard_map(
        per_device,
        mesh=mesh,
        in_specs=placed,
        out_specs=(P("dp", "seq", None), P("dp", "seq", None), P("dp", "seq")),
        check_vma=False,
    )
```

```python
import functools
import math

import jax
import jax.numpy as jnp
import numpy as np
from jax import lax
from jax.experimental import pallas as pl
from jax.experimental.pallas import tpu as pltpu
from jax.sharding import PartitionSpec as P

F32, BF16, I32 = jnp.float32, jnp.bfloat16, jnp.int32
MESH = pl.DeviceIdType.MESH
VMEM_BYTES = 58 * 2**20


def spectrum_of(values):
    n = len(values)
    if n == 1:
        return [(values[0], None)]
    even, odd = spectrum_of(values[0::2]), spectrum_of(values[1::2])
    result = [None] * n
    for k in range(n // 2):
        angle = math.pi * (2 * k + 1) / (2 * n)
        c, s = math.cos(angle), -math.sin(angle)
        (er, ei), (hr, hi) = even[k], odd[k]
        if ei is None:
            tr, ti = c * hr, s * hr
            result[k], result[n - 1 - k] = (er + tr, ti), (er - tr, ti)
            continue
        tr, ti = c * hr - s * hi, c * hi + s * hr
        result[k], result[n - 1 - k] = (er + tr, ei + ti), (er - tr, ti - ei)
    return result


def values_of(spectrum):
    n = len(spectrum)
    if n == 1:
        return [spectrum[0][0]]
    even, odd = [], []
    for k in range(n // 2):
        angle = math.pi * (2 * k + 1) / (2 * n)
        c, s = math.cos(angle), math.sin(angle)
        (zr, zi), (pr, pi) = spectrum[k], spectrum[n - 1 - k]
        dr, di = zr - pr, zi + pi
        even.append((zr + pr, zi - pi))
        odd.append((c * dr - s * di, c * di + s * dr))
    result = [None] * n
    result[0::2], result[1::2] = values_of(even), values_of(odd)
    return result


@functools.lru_cache
def tables(blocks, rows):
    k1 = np.arange(blocks)[:, None, None]
    k2 = np.arange(rows)[None, :, None]
    n1 = np.arange(rows)[None, None, :]
    length = 2 * blocks * rows
    phase = (np.pi / length) * ((2 * k1 + 1) * n1 + 2 * blocks * 2 * (k2 * n1 % rows))
    c, s = np.cos(phase), np.sin(phase)
    table = np.concatenate([np.concatenate([c, s], 2), np.concatenate([-s, c], 2)], 1)
    back = np.swapaxes(table, 1, 2) / (blocks * rows)
    return table.astype(jnp.bfloat16), back.astype(jnp.bfloat16)


def kernel(
    n_dp,
    n_seq,
    order,
    owners_in,
    gate,
    conv,
    upstream,
    taps,
    table_in,
    back_in,
    gate_out,
    rows_out,
    filter_out,
    place_of,
    gate_v,
    up_v,
    mixed_v,
    sig_got,
    own_got,
    conv_got,
    taps_got,
    mixed_got,
    table,
    back_table,
    pair_a,
    specs,
    turned,
    sig_time,
    sig_send,
    back_time,
    starts,
    slot_of,
    row_of,
    packed,
    rows_send,
    filt_send,
    parts_got,
    send_sem,
    recv_sem,
    local_sem,
    ring_send,
    ring_recv,
):
    dp, seq = lax.axis_index("dp"), lax.axis_index("seq")
    rows = gate_v.shape[0]
    lanes = conv_got.shape[2]
    tile = 16
    slot = rows_send.shape[1] // n_seq
    side = math.isqrt(n_seq // 2)

    loads = [
        pltpu.make_async_copy(a, b, local_sem.at[i])
        for i, (a, b) in enumerate(
            (
                (gate, gate_v),
                (upstream, up_v),
                (table_in, table),
                (back_in, back_table),
            )
        )
    ]
    for load in loads:
        load.start()

    barrier = pltpu.get_barrier_semaphore()

    @pl.loop(1, n_seq)
    def _(hop):
        to = lax.rem(seq + hop, n_seq)
        pl.semaphore_signal(barrier, inc=1, device_id=(dp, to), device_id_type=MESH)

    @pl.loop(1, n_dp)
    def _(hop):
        to = lax.rem(dp + hop, n_dp)
        pl.semaphore_signal(barrier, inc=1, device_id=(to, seq), device_id_type=MESH)

    pl.semaphore_wait(barrier, n_seq - 1 + n_dp - 1)

    def columns(ref, which):
        return ref.at[:, pl.ds(pl.multiple_of(which * lanes, lanes), lanes)]

    core, place_x, place_y = seq % 2, seq // 2 % side, seq // (2 * side)
    odd, sign = (place_x + place_y) % 2, 1 - 2 * core

    def partner(hop):
        u, v = hop // 2 % side, hop // (2 * side)
        dx, dy = odd * v + (1 - odd) * u, odd * u + (1 - odd) * v
        y, x = (place_y + side + sign * dy) % side, (place_x + side + sign * dx) % side
        return (y * side + x) * 2 + (core + hop) % 2

    def remote(i, source, target, to):
        return pltpu.make_async_remote_copy(
            src_ref=source,
            dst_ref=target,
            send_sem=send_sem.at[i],
            recv_sem=recv_sem.at[i],
            device_id=(dp, to),
            device_id_type=MESH,
        )

    def exchange(i, source, target):
        @pl.loop(1, n_seq)
        def _(hop):
            to = partner(hop)
            remote(i, source(to), target, to).start()

        pltpu.make_async_copy(source(seq), target, recv_sem.at[i]).start()

    def arrived(i, ref):
        pltpu.make_async_copy(ref, ref, recv_sem.at[i]).wait()

    def left(i, ref):
        part = ref.at[pl.ds(0, ref.shape[0] - ref.shape[0] // n_seq)]
        pltpu.make_async_copy(part, part, send_sem.at[i]).wait()

    share = taps.at[pl.ds(pl.multiple_of(dp * tile, tile), tile)]
    exchange(2, lambda to: columns(share, to), taps_got.at[dp, seq])
    exchange(0, lambda to: owners_in, own_got.at[pl.ds(seq, 1)])
    exchange(1, lambda to: columns(conv, to), conv_got.at[seq])
    loads[0].wait()
    loads[1].wait()

    @pl.loop(0, rows // tile)
    def _(i):
        at = pl.ds(pl.multiple_of(i * tile, tile), tile)
        mixed_v[at, :] = (up_v[at, :].astype(F32) * gate_v[at, :].astype(F32)).astype(BF16)

    exchange(3, lambda to: columns(mixed_v, to), mixed_got.at[seq])

    def ring(step):
        halves = step == n_dp // 2 - 1
        parts = (pl.ds(0, n_seq // 2), pl.ds(n_seq // 2, n_seq // 2)) if halves else (pl.ds(0, n_seq),) * 2
        copies = []
        for way, turn in enumerate((1, -1)):
            held = taps_got.at[lax.rem(dp - turn * step + n_dp, n_dp), parts[way]]
            copies.append(
                pltpu.make_async_remote_copy(
                    src_ref=held,
                    dst_ref=held,
                    send_sem=ring_send.at[2 * step + way],
                    recv_sem=ring_recv.at[2 * step + way],
                    device_id=(lax.rem(dp + turn + n_dp, n_dp), seq),
                    device_id_type=MESH,
                )
            )
        return copies

    rings = [ring(step) for step in range(n_dp // 2)]

    def send_on(step):
        for copy in rings[step]:
            copy.start()

    def met(step):
        for copy in rings[step]:
            copy.wait_recv()

    arrived(2, taps_got.at[dp])
    send_on(0)

    def transform(load, into, lane):
        @pl.loop(0, rows // tile)
        def _(i):
            at = pl.ds(pl.multiple_of(i * tile, tile), tile)
            low = pl.ds(pl.multiple_of(rows + i * tile, tile), tile)
            found = spectrum_of([load(q, at, i).astype(F32) for q in range(n_seq)])
            for k in range(n_seq):
                into[k, at, lane : lane + lanes] = found[k][0].astype(BF16)
                into[k, low, lane : lane + lanes] = found[k][1].astype(BF16)

    def invert(lane, put):
        @pl.loop(0, rows // tile)
        def _(i):
            at = pl.ds(pl.multiple_of(i * tile, tile), tile)
            low = pl.ds(pl.multiple_of(rows + i * tile, tile), tile)
            found = values_of(
                [
                    (turned[k, at, lane : lane + lanes], turned[k, low, lane : lane + lanes])
                    for k in range(n_seq)
                ]
            )
            for q in range(n_seq):
                put(q, at, i, found[q].astype(BF16))

    @pl.loop(0, n_seq)
    def _(q):
        found = 0
        for p in range(n_seq):
            found = jnp.where(order[p] == q, p, found)
        place_of[q] = found

    arrived(0, own_got)
    owner_ids = lax.broadcasted_iota(I32, (n_seq, rows), 0)
    wide = lax.broadcasted_iota(I32, (n_seq, n_seq * slot), 1)
    wide_block, wide_slot = wide // slot, wide % slot
    above = lax.broadcasted_iota(I32, (rows, rows), 0)
    beside = lax.broadcasted_iota(I32, (rows, rows), 1)
    earlier = jnp.where(above < beside, 1.0, 0.0).astype(BF16)

    def place(p, carry):
        so_far, first = carry
        owner = own_got[pl.ds(p, 1), :]
        hits = jnp.where(owner == owner_ids, 1.0, 0.0)
        count = jnp.sum(hits, axis=1, keepdims=True).astype(I32)
        mine = jnp.logical_and(wide_block == p, wide_slot < count)
        return so_far + count, jnp.where(mine, so_far + wide_slot, first)

    _, first = lax.fori_loop(
        0,
        n_seq,
        place,
        (jnp.zeros((n_seq, 1), I32), jnp.full((n_seq, n_seq * slot), -1, I32)),
    )
    starts[...] = first
    met(0)
    send_on(1)

    @pl.loop(0, n_seq, unroll=4)
    def _(p):
        owner = own_got[pl.ds(p, 1), :]
        hits = jnp.where(owner == owner_ids, 1.0, 0.0)
        before = jnp.dot(hits.astype(BF16), earlier, preferred_element_type=F32)
        rank = jnp.sum(hits * before, axis=0, keepdims=True).astype(I32)
        place_ids = lax.broadcasted_iota(I32, (n_seq * slot, rows), 0)
        slot_of[p] = jnp.where(owner * slot + rank == place_ids, 1.0, 0.0).astype(BF16)

    met(1)
    send_on(2)

    @pl.loop(0, n_seq, unroll=4)
    def _(o):
        row_ids = lax.broadcasted_iota(I32, (n_seq * slot, n_seq * slot), 0)
        row_of[o] = jnp.where(starts[pl.ds(o, 1), :] == row_ids, 1.0, 0.0).astype(BF16)

    met(2)
    send_on(3)
    arrived(1, conv_got)
    transform(lambda q, at, i: conv_got[place_of[q], at, :], pair_a, 0)
    met(3)
    transform(lambda q, at, i: taps_got[i, q], pair_a, lanes)
    loads[2].wait()
    loads[3].wait()

    @pl.loop(0, n_seq, unroll=16)
    def _(k):
        both = jnp.dot(table[k], pair_a[k], preferred_element_type=F32)
        specs[k] = both
        xr, xi = both[:rows, :lanes], both[rows:, :lanes]
        tr, ti = both[:rows, lanes:], both[rows:, lanes:]
        made = jnp.concatenate([xr * tr - xi * ti, xr * ti + xi * tr], axis=0)
        turned[k, :, :lanes] = jnp.dot(
            back_table[k], made.astype(BF16), preferred_element_type=F32
        )

    def put_signal(q, at, i, found):
        sig_time[q, at, :] = found

    invert(0, put_signal)

    @pl.loop(0, n_seq)
    def _(p):
        sig_send[p] = sig_time[order[p]]

    exchange(4, lambda to: sig_send.at[to], columns(sig_got, seq))

    arrived(3, mixed_got)
    transform(lambda q, at, i: mixed_got[place_of[q], at, :], pair_a, 0)

    @pl.loop(0, n_seq, unroll=16)
    def _(k):
        mixed = jnp.dot(table[k], pair_a[k, :, :lanes], preferred_element_type=F32)
        mr, mi = mixed[:rows], mixed[rows:]
        xr, xi = specs[k, :rows, :lanes], specs[k, rows:, :lanes]
        tr, ti = specs[k, :rows, lanes:], specs[k, rows:, lanes:]
        made = jnp.concatenate([tr * mr + ti * mi, tr * mi - ti * mr], axis=0)
        turned[k, :, :lanes] = jnp.dot(
            back_table[k], made.astype(BF16), preferred_element_type=F32
        )
        cross = jnp.concatenate([xr * mr + xi * mi, xr * mi - xi * mr], axis=0)
        pair_a[k, :, lanes:] = cross.astype(BF16)

    def put_back(q, at, i, found):
        back_time[q, at, :] = found

    invert(0, put_back)

    @pl.loop(0, n_seq, unroll=8)
    def _(p):
        found = jnp.dot(slot_of[p], back_time[order[p]], preferred_element_type=F32)
        at = pl.ds(pl.multiple_of(p * slot, slot), slot)
        packed[:, at, :] = found.reshape(n_seq, slot, lanes)

    together = 8

    @pl.loop(0, n_seq // together)
    def _(group):
        partners = [partner(group * together + step) for step in range(together)]
        for to in partners:
            found = jnp.dot(row_of[to], packed[to].astype(BF16), preferred_element_type=F32)
            rows_send[to] = found.astype(BF16)
        for step, to in enumerate(partners):
            copy = remote(5, rows_send.at[to], columns(rows_out, seq), to)
            if step:
                copy.start()
                continue
            pl.when(group > 0)(copy.start)

            @pl.when(group == 0)
            def _():
                own = rows_send.at[seq]
                pltpu.make_async_copy(own, columns(rows_out, seq), recv_sem.at[5]).start()

    per = n_seq // n_dp

    def put_filter(q, at, i, found):
        down = pl.ds(pl.multiple_of((q % per) * rows + i * tile, tile), tile)
        filt_send[q // per, down, :] = found

    @pl.loop(0, n_seq, unroll=16)
    def _(k):
        turned[k, :, lanes:] = jnp.dot(
            back_table[k], pair_a[k, :, lanes:], preferred_element_type=F32
        )

    invert(lanes, put_filter)

    @pl.loop(1, n_dp)
    def _(hop):
        to = lax.rem(dp + hop, n_dp)
        pltpu.make_async_remote_copy(
            src_ref=filt_send.at[to],
            dst_ref=parts_got.at[dp],
            send_sem=send_sem.at[6],
            recv_sem=recv_sem.at[6],
            device_id=(to, seq),
            device_id_type=MESH,
        ).start()

    pltpu.make_async_copy(filt_send.at[dp], parts_got.at[dp], recv_sem.at[6]).start()

    arrived(4, sig_got)

    @pl.loop(0, rows // tile)
    def _(i):
        at = pl.ds(pl.multiple_of(i * tile, tile), tile)
        gate_out[at, :] = (up_v[at, :].astype(F32) * sig_got[at, :].astype(F32)).astype(BF16)

    arrived(6, parts_got)

    @pl.loop(0, per * rows // tile)
    def _(i):
        at = pl.ds(pl.multiple_of(i * tile, tile), tile)
        total = parts_got[0, at, :].astype(F32)
        for z in range(1, n_dp):
            total = total + parts_got[z, at, :].astype(F32)
        filter_out[at, :] = total

    left(0, own_got)
    left(1, conv_got)
    left(2, taps_got.at[dp])
    for copies in rings:
        for copy in copies:
            copy.wait_send()
    left(3, mixed_got)
    left(4, sig_send)
    left(5, rows_send)
    others = filt_send.at[pl.ds(0, n_dp - 1)]
    pltpu.make_async_copy(others, others, send_sem.at[6]).wait()
    arrived(5, rows_out)


def per_device(gate_input, conv_input, grad_output, filter_taps, block_order, owner_rows):
    gate_rows, conv_rows, upstream = gate_input[0], conv_input[0], grad_output[0]
    rows, channels = gate_rows.shape
    n_dp, n_seq = lax.axis_size("dp"), lax.axis_size("seq")
    lanes = channels // n_seq
    cap = 2 * rows
    slot = cap // n_seq
    table, back_table = tables(n_seq, rows)
    anywhere, scalars = pl.BlockSpec(memory_space=pl.ANY), pl.BlockSpec(memory_space=pltpu.SMEM)
    full = (n_seq, rows, lanes)
    square = (n_seq, 2 * rows, 2 * lanes)
    parts = (n_dp, n_seq * rows // n_dp, lanes)
    scratch = [
        pltpu.SMEM((n_seq,), I32),
        *[pltpu.VMEM((rows, channels), BF16)] * 4,
        pltpu.VMEM((n_seq, rows), I32),
        pltpu.VMEM(full, BF16),
        pltpu.VMEM((n_dp, n_seq, rows // n_dp, lanes), BF16),
        pltpu.VMEM(full, BF16),
        *[pltpu.VMEM((n_seq, 2 * rows, 2 * rows), BF16)] * 2,
        pltpu.VMEM(square, BF16),
        pltpu.VMEM(square, F32),
        pltpu.VMEM(square, F32),
        *[pltpu.VMEM(full, BF16)] * 3,
        pltpu.VMEM((n_seq, cap), I32),
        pltpu.VMEM((n_seq, cap, rows), BF16),
        pltpu.VMEM((n_seq, cap, cap), BF16),
        pltpu.VMEM((n_seq, cap, lanes), F32),
        pltpu.VMEM((n_seq, cap, lanes), BF16),
        pltpu.VMEM(parts, BF16),
        pltpu.VMEM(parts, BF16),
        pltpu.SemaphoreType.DMA((7,)),
        pltpu.SemaphoreType.DMA((7,)),
        pltpu.SemaphoreType.DMA((4,)),
        pltpu.SemaphoreType.DMA((n_dp,)),
        pltpu.SemaphoreType.DMA((n_dp,)),
    ]
    grad_gate, returned, grad_filter = pl.pallas_call(
        functools.partial(kernel, n_dp, n_seq),
        out_shape=(
            pltpu.VMEM((rows, channels), BF16),
            pltpu.VMEM((cap, channels), BF16),
            pltpu.VMEM(parts[1:], F32),
        ),
        in_specs=[scalars] + [anywhere] * 7,
        out_specs=(pl.BlockSpec(memory_space=pltpu.VMEM),) * 3,
        scratch_shapes=scratch,
        compiler_params=pltpu.CompilerParams(
            collective_id=0, has_side_effects=True, vmem_limit_bytes=VMEM_BYTES
        ),
        name="conv_backward",
    )(
        block_order,
        owner_rows,
        gate_rows,
        conv_rows,
        upstream,
        filter_taps,
        jnp.asarray(table),
        jnp.asarray(back_table),
    )
    return grad_gate[None], returned[None], grad_filter


def solution(mesh):
    placed = (
        P("dp", "seq", None),
        P("dp", "seq", None),
        P("dp", "seq", None),
        P("seq", None),
        P(),
        P("dp", "seq"),
    )
    return jax.shard_map(
        per_device,
        mesh=mesh,
        in_specs=placed,
        out_specs=(P("dp", "seq", None), P("dp", "seq", None), P("dp", "seq")),
        check_vma=False,
    )
```

```python
import functools
import math

import jax
import jax.numpy as jnp
import numpy as np
from jax import lax
from jax.experimental import pallas as pl
from jax.experimental.pallas import tpu as pltpu
from jax.sharding import PartitionSpec as P

F32, BF16, I32 = jnp.float32, jnp.bfloat16, jnp.int32
MESH = pl.DeviceIdType.MESH
VMEM_BYTES = 58 * 2**20


def spectrum_of(values):
    n = len(values)
    if n == 1:
        return [(values[0], None)]
    even, odd = spectrum_of(values[0::2]), spectrum_of(values[1::2])
    result = [None] * n
    for k in range(n // 2):
        angle = math.pi * (2 * k + 1) / (2 * n)
        c, s = math.cos(angle), -math.sin(angle)
        (er, ei), (hr, hi) = even[k], odd[k]
        if ei is None:
            tr, ti = c * hr, s * hr
            result[k], result[n - 1 - k] = (er + tr, ti), (er - tr, ti)
            continue
        tr, ti = c * hr - s * hi, c * hi + s * hr
        result[k], result[n - 1 - k] = (er + tr, ei + ti), (er - tr, ti - ei)
    return result


def values_of(spectrum):
    n = len(spectrum)
    if n == 1:
        return [spectrum[0][0]]
    even, odd = [], []
    for k in range(n // 2):
        angle = math.pi * (2 * k + 1) / (2 * n)
        c, s = math.cos(angle), math.sin(angle)
        (zr, zi), (pr, pi) = spectrum[k], spectrum[n - 1 - k]
        dr, di = zr - pr, zi + pi
        even.append((zr + pr, zi - pi))
        odd.append((c * dr - s * di, c * di + s * dr))
    result = [None] * n
    result[0::2], result[1::2] = values_of(even), values_of(odd)
    return result


@functools.lru_cache
def tables(blocks, rows):
    k1 = np.arange(blocks)[:, None, None]
    k2 = np.arange(rows)[None, :, None]
    n1 = np.arange(rows)[None, None, :]
    length = 2 * blocks * rows
    phase = (np.pi / length) * ((2 * k1 + 1) * n1 + 2 * blocks * 2 * (k2 * n1 % rows))
    c, s = np.cos(phase), np.sin(phase)
    table = np.concatenate([np.concatenate([c, s], 2), np.concatenate([-s, c], 2)], 1)
    back = np.swapaxes(table, 1, 2) / (blocks * rows)
    return table.astype(jnp.bfloat16), back.astype(jnp.bfloat16)


def kernel(
    n_dp,
    n_seq,
    order,
    owners_in,
    gate,
    conv,
    upstream,
    taps,
    table_in,
    back_in,
    gate_out,
    rows_out,
    filter_out,
    place_of,
    gate_v,
    up_v,
    mixed_v,
    sig_got,
    own_got,
    conv_got,
    taps_got,
    mixed_got,
    table,
    back_table,
    pair_a,
    specs,
    turned,
    sig_time,
    sig_send,
    back_time,
    starts,
    slot_of,
    row_of,
    packed,
    rows_send,
    filt_send,
    parts_got,
    send_sem,
    recv_sem,
    local_sem,
    ring_send,
    ring_recv,
):
    dp, seq = lax.axis_index("dp"), lax.axis_index("seq")
    rows = gate_v.shape[0]
    lanes = conv_got.shape[2]
    tile = 16
    slot = rows_send.shape[1] // n_seq
    side = math.isqrt(n_seq // 2)

    loads = [
        pltpu.make_async_copy(a, b, local_sem.at[i])
        for i, (a, b) in enumerate(
            (
                (gate, gate_v),
                (upstream, up_v),
                (table_in, table),
                (back_in, back_table),
            )
        )
    ]
    for load in loads:
        load.start()

    barrier = pltpu.get_barrier_semaphore()

    @pl.loop(1, n_seq)
    def _(hop):
        to = lax.rem(seq + hop, n_seq)
        pl.semaphore_signal(barrier, inc=1, device_id=(dp, to), device_id_type=MESH)

    @pl.loop(1, n_dp)
    def _(hop):
        to = lax.rem(dp + hop, n_dp)
        pl.semaphore_signal(barrier, inc=1, device_id=(to, seq), device_id_type=MESH)

    pl.semaphore_wait(barrier, n_seq - 1 + n_dp - 1)

    def columns(ref, which):
        return ref.at[:, pl.ds(pl.multiple_of(which * lanes, lanes), lanes)]

    core, place_x, place_y = seq % 2, seq // 2 % side, seq // (2 * side)
    odd, sign = (place_x + place_y) % 2, 1 - 2 * core

    def partner(hop):
        u, v = hop // 2 % side, hop // (2 * side)
        dx, dy = odd * v + (1 - odd) * u, odd * u + (1 - odd) * v
        y, x = (place_y + side + sign * dy) % side, (place_x + side + sign * dx) % side
        return (y * side + x) * 2 + (core + hop) % 2

    def remote(i, source, target, to):
        return pltpu.make_async_remote_copy(
            src_ref=source,
            dst_ref=target,
            send_sem=send_sem.at[i],
            recv_sem=recv_sem.at[i],
            device_id=(dp, to),
            device_id_type=MESH,
        )

    def exchange(i, source, target):
        @pl.loop(1, n_seq)
        def _(hop):
            to = partner(hop)
            remote(i, source(to), target, to).start()

        pltpu.make_async_copy(source(seq), target, recv_sem.at[i]).start()

    def arrived(i, ref):
        pltpu.make_async_copy(ref, ref, recv_sem.at[i]).wait()

    def left(i, ref):
        part = ref.at[pl.ds(0, ref.shape[0] - ref.shape[0] // n_seq)]
        pltpu.make_async_copy(part, part, send_sem.at[i]).wait()

    share = taps.at[pl.ds(pl.multiple_of(dp * tile, tile), tile)]
    exchange(2, lambda to: columns(share, to), taps_got.at[dp, seq])
    exchange(0, lambda to: owners_in, own_got.at[pl.ds(seq, 1)])
    exchange(1, lambda to: columns(conv, to), conv_got.at[seq])
    loads[0].wait()
    loads[1].wait()

    @pl.loop(0, rows // tile)
    def _(i):
        at = pl.ds(pl.multiple_of(i * tile, tile), tile)
        mixed_v[at, :] = (up_v[at, :].astype(F32) * gate_v[at, :].astype(F32)).astype(BF16)

    exchange(3, lambda to: columns(mixed_v, to), mixed_got.at[seq])

    def ring(step):
        halves = step == n_dp // 2 - 1
        parts = (pl.ds(0, n_seq // 2), pl.ds(n_seq // 2, n_seq // 2)) if halves else (pl.ds(0, n_seq),) * 2
        copies = []
        for way, turn in enumerate((1, -1)):
            held = taps_got.at[lax.rem(dp - turn * step + n_dp, n_dp), parts[way]]
            copies.append(
                pltpu.make_async_remote_copy(
                    src_ref=held,
                    dst_ref=held,
                    send_sem=ring_send.at[2 * step + way],
                    recv_sem=ring_recv.at[2 * step + way],
                    device_id=(lax.rem(dp + turn + n_dp, n_dp), seq),
                    device_id_type=MESH,
                )
            )
        return copies

    rings = [ring(step) for step in range(n_dp // 2)]

    def send_on(step):
        for copy in rings[step]:
            copy.start()

    def met(step):
        for copy in rings[step]:
            copy.wait_recv()

    arrived(2, taps_got.at[dp])
    send_on(0)

    def transform(load, into, lane):
        @pl.loop(0, rows // tile)
        def _(i):
            at = pl.ds(pl.multiple_of(i * tile, tile), tile)
            low = pl.ds(pl.multiple_of(rows + i * tile, tile), tile)
            found = spectrum_of([load(q, at, i).astype(F32) for q in range(n_seq)])
            for k in range(n_seq):
                into[k, at, lane : lane + lanes] = found[k][0].astype(BF16)
                into[k, low, lane : lane + lanes] = found[k][1].astype(BF16)

    def invert(lane, put):
        @pl.loop(0, rows // tile)
        def _(i):
            at = pl.ds(pl.multiple_of(i * tile, tile), tile)
            low = pl.ds(pl.multiple_of(rows + i * tile, tile), tile)
            found = values_of(
                [
                    (turned[k, at, lane : lane + lanes], turned[k, low, lane : lane + lanes])
                    for k in range(n_seq)
                ]
            )
            for q in range(n_seq):
                put(q, at, i, found[q].astype(BF16))

    @pl.loop(0, n_seq)
    def _(q):
        found = 0
        for p in range(n_seq):
            found = jnp.where(order[p] == q, p, found)
        place_of[q] = found

    arrived(0, own_got)
    owner_ids = lax.broadcasted_iota(I32, (n_seq, rows), 0)
    wide = lax.broadcasted_iota(I32, (n_seq, n_seq * slot), 1)
    wide_block, wide_slot = wide // slot, wide % slot
    above = lax.broadcasted_iota(I32, (rows, rows), 0)
    beside = lax.broadcasted_iota(I32, (rows, rows), 1)
    earlier = jnp.where(above < beside, 1.0, 0.0).astype(BF16)

    def place(p, carry):
        so_far, first = carry
        owner = own_got[pl.ds(p, 1), :]
        hits = jnp.where(owner == owner_ids, 1.0, 0.0)
        count = jnp.sum(hits, axis=1, keepdims=True).astype(I32)
        mine = jnp.logical_and(wide_block == p, wide_slot < count)
        return so_far + count, jnp.where(mine, so_far + wide_slot, first)

    _, first = lax.fori_loop(
        0,
        n_seq,
        place,
        (jnp.zeros((n_seq, 1), I32), jnp.full((n_seq, n_seq * slot), -1, I32)),
    )
    starts[...] = first
    met(0)
    send_on(1)

    @pl.loop(0, n_seq, unroll=4)
    def _(p):
        owner = own_got[pl.ds(p, 1), :]
        hits = jnp.where(owner == owner_ids, 1.0, 0.0)
        before = jnp.dot(hits.astype(BF16), earlier, preferred_element_type=F32)
        rank = jnp.sum(hits * before, axis=0, keepdims=True).astype(I32)
        place_ids = lax.broadcasted_iota(I32, (n_seq * slot, rows), 0)
        slot_of[p] = jnp.where(owner * slot + rank == place_ids, 1.0, 0.0).astype(BF16)

    met(1)
    send_on(2)

    @pl.loop(0, n_seq, unroll=4)
    def _(o):
        row_ids = lax.broadcasted_iota(I32, (n_seq * slot, n_seq * slot), 0)
        row_of[o] = jnp.where(starts[pl.ds(o, 1), :] == row_ids, 1.0, 0.0).astype(BF16)

    met(2)
    send_on(3)
    arrived(1, conv_got)
    transform(lambda q, at, i: conv_got[place_of[q], at, :], pair_a, 0)
    met(3)
    transform(lambda q, at, i: taps_got[i, q], pair_a, lanes)
    loads[2].wait()
    loads[3].wait()

    @pl.loop(0, n_seq, unroll=32)
    def _(k):
        both = jnp.dot(table[k], pair_a[k], preferred_element_type=F32)
        specs[k] = both
        xr, xi = both[:rows, :lanes], both[rows:, :lanes]
        tr, ti = both[:rows, lanes:], both[rows:, lanes:]
        made = jnp.concatenate([xr * tr - xi * ti, xr * ti + xi * tr], axis=0)
        turned[k, :, :lanes] = jnp.dot(
            back_table[k], made.astype(BF16), preferred_element_type=F32
        )

    def put_signal(q, at, i, found):
        sig_time[q, at, :] = found

    invert(0, put_signal)

    @pl.loop(0, n_seq)
    def _(p):
        sig_send[p] = sig_time[order[p]]

    exchange(4, lambda to: sig_send.at[to], columns(sig_got, seq))

    arrived(3, mixed_got)
    transform(lambda q, at, i: mixed_got[place_of[q], at, :], pair_a, 0)

    @pl.loop(0, n_seq, unroll=32)
    def _(k):
        mixed = jnp.dot(table[k], pair_a[k, :, :lanes], preferred_element_type=F32)
        mr, mi = mixed[:rows], mixed[rows:]
        xr, xi = specs[k, :rows, :lanes], specs[k, rows:, :lanes]
        tr, ti = specs[k, :rows, lanes:], specs[k, rows:, lanes:]
        made = jnp.concatenate([tr * mr + ti * mi, tr * mi - ti * mr], axis=0)
        turned[k, :, :lanes] = jnp.dot(
            back_table[k], made.astype(BF16), preferred_element_type=F32
        )
        cross = jnp.concatenate([xr * mr + xi * mi, xr * mi - xi * mr], axis=0)
        pair_a[k, :, lanes:] = cross.astype(BF16)

    def put_back(q, at, i, found):
        back_time[q, at, :] = found

    invert(0, put_back)

    @pl.loop(0, n_seq, unroll=16)
    def _(p):
        found = jnp.dot(slot_of[p], back_time[order[p]], preferred_element_type=F32)
        at = pl.ds(pl.multiple_of(p * slot, slot), slot)
        packed[:, at, :] = found.reshape(n_seq, slot, lanes)

    together = 16

    @pl.loop(0, n_seq // together)
    def _(group):
        partners = [partner(group * together + step) for step in range(together)]
        for to in partners:
            found = jnp.dot(row_of[to], packed[to].astype(BF16), preferred_element_type=F32)
            rows_send[to] = found.astype(BF16)
        for step, to in enumerate(partners):
            copy = remote(5, rows_send.at[to], columns(rows_out, seq), to)
            if step:
                copy.start()
                continue
            pl.when(group > 0)(copy.start)

            @pl.when(group == 0)
            def _():
                own = rows_send.at[seq]
                pltpu.make_async_copy(own, columns(rows_out, seq), recv_sem.at[5]).start()

    per = n_seq // n_dp

    def put_filter(q, at, i, found):
        down = pl.ds(pl.multiple_of((q % per) * rows + i * tile, tile), tile)
        filt_send[q // per, down, :] = found

    @pl.loop(0, n_seq, unroll=32)
    def _(k):
        turned[k, :, lanes:] = jnp.dot(
            back_table[k], pair_a[k, :, lanes:], preferred_element_type=F32
        )

    invert(lanes, put_filter)

    @pl.loop(1, n_dp)
    def _(hop):
        to = lax.rem(dp + hop, n_dp)
        pltpu.make_async_remote_copy(
            src_ref=filt_send.at[to],
            dst_ref=parts_got.at[dp],
            send_sem=send_sem.at[6],
            recv_sem=recv_sem.at[6],
            device_id=(to, seq),
            device_id_type=MESH,
        ).start()

    pltpu.make_async_copy(filt_send.at[dp], parts_got.at[dp], recv_sem.at[6]).start()

    arrived(4, sig_got)

    @pl.loop(0, rows // tile)
    def _(i):
        at = pl.ds(pl.multiple_of(i * tile, tile), tile)
        gate_out[at, :] = (up_v[at, :].astype(F32) * sig_got[at, :].astype(F32)).astype(BF16)

    arrived(6, parts_got)

    @pl.loop(0, per * rows // tile)
    def _(i):
        at = pl.ds(pl.multiple_of(i * tile, tile), tile)
        total = parts_got[0, at, :].astype(F32)
        for z in range(1, n_dp):
            total = total + parts_got[z, at, :].astype(F32)
        filter_out[at, :] = total

    left(0, own_got)
    left(1, conv_got)
    left(2, taps_got.at[dp])
    for copies in rings:
        for copy in copies:
            copy.wait_send()
    left(3, mixed_got)
    left(4, sig_send)
    left(5, rows_send)
    others = filt_send.at[pl.ds(0, n_dp - 1)]
    pltpu.make_async_copy(others, others, send_sem.at[6]).wait()
    arrived(5, rows_out)


def per_device(gate_input, conv_input, grad_output, filter_taps, block_order, owner_rows):
    gate_rows, conv_rows, upstream = gate_input[0], conv_input[0], grad_output[0]
    rows, channels = gate_rows.shape
    n_dp, n_seq = lax.axis_size("dp"), lax.axis_size("seq")
    lanes = channels // n_seq
    cap = 2 * rows
    slot = cap // n_seq
    table, back_table = tables(n_seq, rows)
    anywhere, scalars = pl.BlockSpec(memory_space=pl.ANY), pl.BlockSpec(memory_space=pltpu.SMEM)
    full = (n_seq, rows, lanes)
    square = (n_seq, 2 * rows, 2 * lanes)
    parts = (n_dp, n_seq * rows // n_dp, lanes)
    scratch = [
        pltpu.SMEM((n_seq,), I32),
        *[pltpu.VMEM((rows, channels), BF16)] * 4,
        pltpu.VMEM((n_seq, rows), I32),
        pltpu.VMEM(full, BF16),
        pltpu.VMEM((n_dp, n_seq, rows // n_dp, lanes), BF16),
        pltpu.VMEM(full, BF16),
        *[pltpu.VMEM((n_seq, 2 * rows, 2 * rows), BF16)] * 2,
        pltpu.VMEM(square, BF16),
        pltpu.VMEM(square, F32),
        pltpu.VMEM(square, F32),
        *[pltpu.VMEM(full, BF16)] * 3,
        pltpu.VMEM((n_seq, cap), I32),
        pltpu.VMEM((n_seq, cap, rows), BF16),
        pltpu.VMEM((n_seq, cap, cap), BF16),
        pltpu.VMEM((n_seq, cap, lanes), F32),
        pltpu.VMEM((n_seq, cap, lanes), BF16),
        pltpu.VMEM(parts, BF16),
        pltpu.VMEM(parts, BF16),
        pltpu.SemaphoreType.DMA((7,)),
        pltpu.SemaphoreType.DMA((7,)),
        pltpu.SemaphoreType.DMA((4,)),
        pltpu.SemaphoreType.DMA((n_dp,)),
        pltpu.SemaphoreType.DMA((n_dp,)),
    ]
    grad_gate, returned, grad_filter = pl.pallas_call(
        functools.partial(kernel, n_dp, n_seq),
        out_shape=(
            pltpu.VMEM((rows, channels), BF16),
            pltpu.VMEM((cap, channels), BF16),
            pltpu.VMEM(parts[1:], F32),
        ),
        in_specs=[scalars] + [anywhere] * 7,
        out_specs=(pl.BlockSpec(memory_space=pltpu.VMEM),) * 3,
        scratch_shapes=scratch,
        compiler_params=pltpu.CompilerParams(
            collective_id=0, has_side_effects=True, vmem_limit_bytes=VMEM_BYTES
        ),
        name="conv_backward",
    )(
        block_order,
        owner_rows,
        gate_rows,
        conv_rows,
        upstream,
        filter_taps,
        jnp.asarray(table),
        jnp.asarray(back_table),
    )
    return grad_gate[None], returned[None], grad_filter


def solution(mesh):
    placed = (
        P("dp", "seq", None),
        P("dp", "seq", None),
        P("dp", "seq", None),
        P("seq", None),
        P(),
        P("dp", "seq"),
    )
    return jax.shard_map(
        per_device,
        mesh=mesh,
        in_specs=placed,
        out_specs=(P("dp", "seq", None), P("dp", "seq", None), P("dp", "seq")),
        check_vma=False,
    )
```
